256 devices in a mesh: ctx: 32 (over z, x), tp: 8 (over y, core).
Axes of the slice: x: 4, y: 4, z: 8, core: 2. Of those that a mesh axis runs over, the one named last changes fastest.
Arguments:
- queries: bfloat16 [16384, 64, 128], P('ctx', 'tp'), may hold values from -6 to 6
- key_rows: bfloat16 [16384, 8, 128], P('ctx', 'tp'), may hold values from -6 to 6
- value_rows: bfloat16 [16384, 8, 128], P('ctx', 'tp'), may hold values from -6 to 6
- segments: int32 [128], replicated, may hold values from 0 to 15, never falling along the last dimension, each value on 1 to 72 neighbouring positions
- gate_input: bfloat16 [16384, 8192], P('ctx', 'tp'), may hold values from -360 to 360
- state_proj: bfloat16 [16384, 2, 8, 128], P('ctx', None, 'tp'), may hold values from -1.5 to 1.5
- step_input: float32 [16384, 128], P('ctx', 'tp'), may hold values from -3 to 3
- step_bias: float32 [128], P('tp'), may hold values from -1 to 1
- decay_rate: float32 [128], P('tp'), may hold values from 6.1035157e-06 to 0.05
- skip_gain: float32 [128], P('tp'), may hold values from 0.5 to 1.5
- conv_input: float32 [4, 8192], P(None, 'tp'), may hold values from -3 to 3
- conv_state: float32 [4, 2, 8, 128], P(None, None, 'tp'), may hold values from -3 to 3
- norm_gain: float32 [8192], P('tp'), may hold values from 0.5 to 1.5
Outputs:
- attention_out: bfloat16 [16384, 8192], P('ctx', 'tp')
- mixer_out: bfloat16 [16384, 8192], P('ctx', 'tp')
The draws below stay inside these ranges and needn't reach their ends.
Inputs may be any that keep to these rules, and one draw needn't show every extreme that they name: `segments`: document numbers of the blocks of 128 tokens never fall; each document spans 1 to 72 whole blocks, and one spans exactly 72.
All inputs are finite; a program needn't handle non-finite values.
Results may differ from the reference program's by a relative error of at most 0.0075.
Values may be sent and summed in bfloat16 or wider, within the bound.
A program may use at most 128 MiB of HBM per device.

```python
import math
import jax
import jax.numpy as jnp
import numpy as np
from jax import lax

HEADS = 64
KV_HEADS = 8
HEAD_DIM = 128
SSM_HEADS = 128
SSM_HEAD_DIM = 64
STATE = 128
GROUPS = 8
CONV_TAPS = 4
BLOCK = 128
TOKENS = 16384
NBLOCKS = 128
DOCS = 16
DOC_MOST = 72


def draw_queries(key, part):
    key = jax.random.fold_in(key, 11)
    dims_all = (TOKENS, HEADS, HEAD_DIM)
    values = jnp.clip(2.5 * jax.random.normal(key, dims_all, jnp.float32), -6.0, 6.0)
    return values.astype(jnp.bfloat16)


def draw_key_rows(key, part):
    key = jax.random.fold_in(key, 12)
    dims_all = (TOKENS, KV_HEADS, HEAD_DIM)
    values = jnp.clip(jax.random.normal(key, dims_all, jnp.float32), -6.0, 6.0)
    return values.astype(jnp.bfloat16)


def draw_gate_input(key, part):
    key = jax.random.fold_in(key, 13)
    noise_key, col_key, row_key = jax.random.split(key, 3)
    channels = SSM_HEADS * SSM_HEAD_DIM
    ramp = jnp.exp(math.log(3.0) * jnp.arange(channels, dtype=jnp.float32) / (channels - 1))
    ramp = ramp * jnp.exp(jax.random.uniform(col_key, (channels,), jnp.float32, 0.0, math.log(3.0)))
    row_scale = jnp.exp(jax.random.uniform(row_key, (TOKENS, 1), jnp.float32, 0.0, math.log(10.0)))
    ground = jnp.clip(jax.random.normal(noise_key, (TOKENS, channels), jnp.float32), -4.0, 4.0)
    return (ground * row_scale * ramp[None, :]).astype(jnp.bfloat16)


def steps_of(stream_key, dims, shards, low, top_value):
    def one(dim, blocks):
        steps = jax.random.uniform(jax.random.fold_in(jax.random.fold_in(stream_key, 6), dim), (blocks,), jnp.float32, low / len(shards), top_value / len(shards))
        return jnp.repeat(jnp.exp(steps), dims[dim] // blocks).reshape((-1,) + (1,) * (len(dims) - dim - 1))

    level = one(*shards[0])
    for cut in shards[1:]:
        level = level * one(*cut)
    return level


def length_profile(count, total, reach, lean):
    loads = [(1 << 20) // math.isqrt(standing ** lean) + 1 for standing in range(2, count + 1)]
    spare, counts = total - reach - (count - 1), [1] * (count - 1)
    while spare > 0:
        free = [i for i in range(count - 1) if counts[i] < reach]
        whole, left = sum([loads[i] for i in free]), spare
        for i in free:
            more = min(reach - counts[i], max(1, left * loads[i] // whole), spare)
            counts[i] = counts[i] + more
            spare = spare - more
    return np.array([reach] + counts)


def uneven_parts(stream_key, amount, total, bound, slope):
    if amount == 2:
        one = jax.random.randint(stream_key, (), max(1, total - bound), min(bound, total - 1) + 1)
        return jnp.stack([one, total - one])
    sizes = jnp.asarray(length_profile(amount, total, bound, slope), jnp.int32)
    couples = (amount - 1) // 2
    giver, sink = sizes[1:1 + 2 * couples:2], sizes[2:2 + 2 * couples:2]
    margin = jnp.minimum(giver - 1, bound - sink)
    passed = jax.random.randint(jax.random.fold_in(stream_key, 1), (couples,), 0, 1 << 20) % (margin + 1)
    sizes = sizes.at[1:1 + 2 * couples:2].set(giver - passed).at[2:2 + 2 * couples:2].set(sink + passed)
    return sizes[jax.random.permutation(jax.random.fold_in(stream_key, 2), amount)]


def centred(rng, extent, spread, limit, cuts=(), kind=jnp.bfloat16):
    entries = spread * jax.random.normal(rng, extent, jnp.float32)
    if cuts:
        entries = entries * steps_of(rng, extent, cuts, -0.22, 0.18)
    return jnp.clip(entries, -limit, limit).astype(kind)


def setup_inputs(seed: int = 0) -> dict:
    key_list = jax.random.split(jax.random.key(seed), 14)
    queries = draw_queries(jax.random.fold_in(key_list[13], 71), 0)
    key_rows = draw_key_rows(jax.random.fold_in(key_list[13], 71), 0)
    value_rows = centred(key_list[2], (TOKENS, KV_HEADS, HEAD_DIM), 1.0, 6.0, ((0, 32), (1, 8)))
    segments = jnp.searchsorted(jnp.cumsum(uneven_parts(key_list[3], DOCS, NBLOCKS, DOC_MOST, 2)), jnp.arange(NBLOCKS), side="right").astype(jnp.int32)
    gate_input = draw_gate_input(jax.random.fold_in(key_list[13], 71), 0)
    state_proj = centred(key_list[5], (TOKENS, 2, GROUPS, STATE), 0.25, 1.5, ((0, 32), (2, 8)))
    step_input = centred(key_list[6], (TOKENS, SSM_HEADS), 0.5, 3.0, ((0, 32), (1, 8)), jnp.float32)
    step_bias = jnp.clip(jax.random.uniform(key_list[7], (SSM_HEADS,), jnp.float32, -1.0, 1.0) * steps_of(key_list[7], (SSM_HEADS,), ((0, 8),), -0.4, 0.0), -1.0, 1.0)
    decay_rate = jnp.clip(jnp.exp(math.log(0.05) - 9.010913 * jax.random.uniform(key_list[8], (SSM_HEADS,), jnp.float32) ** steps_of(key_list[8], (SSM_HEADS,), ((0, 8),), -0.2, 0.2)), 6.10351571594947e-06, 0.05)
    skip_gain = jnp.clip(0.5 + 1.0 * jax.random.uniform(key_list[9], (SSM_HEADS,), jnp.float32) ** steps_of(key_list[9], (SSM_HEADS,), ((0, 8),), -0.2, 0.2), 0.5, 1.5)
    conv_input = centred(key_list[10], (CONV_TAPS, SSM_HEADS * SSM_HEAD_DIM), CONV_TAPS ** -0.5, 3.0, ((1, 8),), jnp.float32)
    conv_state = centred(key_list[11], (CONV_TAPS, 2, GROUPS, STATE), CONV_TAPS ** -0.5, 3.0, ((2, 8),), jnp.float32)
    norm_gain = jnp.clip(1.0 + 0.1 * jax.random.normal(key_list[12], (SSM_HEADS * SSM_HEAD_DIM,), jnp.float32), 0.5, 1.5)
    return {"queries": queries, "key_rows": key_rows, "value_rows": value_rows, "segments": segments, "gate_input": gate_input, "state_proj": state_proj, "step_input": step_input, "step_bias": step_bias, "decay_rate": decay_rate, "skip_gain": skip_gain, "conv_input": conv_input, "conv_state": conv_state, "norm_gain": norm_gain}


full_prec = lax.Precision.HIGHEST
norm_eps = 1e-05

def token_segments(segments, positions):
    block_total = segments.shape[0]
    before = jnp.concatenate([jnp.zeros((1,), jnp.int32), segments[:-1]])
    increments = segments - before
    block_starts = jnp.arange(block_total, dtype=jnp.int32) * BLOCK
    reached = (positions[:, None] >= block_starts[None, :]).astype(jnp.int32)
    return lax.optimization_barrier(jnp.sum(reached * increments[None, :], axis=1)).astype(jnp.int32)

def attention_layer(queries, key_rows, value_rows, segments):
    group_size = HEADS // KV_HEADS
    block_rows = min(256, TOKENS)
    window = min(TOKENS, DOC_MOST * BLOCK + block_rows)
    score_scale = 1.0 / math.sqrt(HEAD_DIM)

    def one_block(block_id):
        first_row = (block_id * block_rows).astype(jnp.int32)
        query_blk = lax.dynamic_slice_in_dim(queries, first_row, block_rows, 0).astype(jnp.float32)
        query_blk = query_blk.reshape(block_rows, KV_HEADS, group_size, HEAD_DIM)
        key_first = jnp.clip(first_row + block_rows - window, 0, TOKENS - window).astype(jnp.int32)
        key_blk = lax.dynamic_slice_in_dim(key_rows, key_first, window, 0).astype(jnp.float32)
        value_blk = lax.dynamic_slice_in_dim(value_rows, key_first, window, 0).astype(jnp.float32)
        query_pos = first_row + jnp.arange(block_rows, dtype=jnp.int32)
        key_pos = key_first + jnp.arange(window, dtype=jnp.int32)
        query_seg = token_segments(segments, query_pos)
        key_seg = token_segments(segments, key_pos)
        allowed = (key_pos[None, :] <= query_pos[:, None]) & (key_seg[None, :] == query_seg[:, None])
        key_mask = allowed[:, None, None, :]
        scores = jnp.einsum('qhgd,khd->qhgk', query_blk, key_blk, precision=full_prec) * score_scale
        row_max = lax.optimization_barrier(jnp.max(jnp.where(key_mask, scores, -1e+30), axis=-1, keepdims=True))
        weights = jnp.where(key_mask, jnp.exp(scores - row_max), 0.0)
        total = lax.optimization_barrier(jnp.sum(weights, axis=-1))
        rounded = lax.optimization_barrier(weights.astype(jnp.bfloat16)).astype(jnp.float32)
        attended = jnp.einsum('qhgk,khd->qhgd', rounded, value_blk, precision=full_prec) / total[..., None]
        return attended.reshape(block_rows, HEADS * HEAD_DIM).astype(jnp.bfloat16)
    blocks = lax.map(one_block, jnp.arange(TOKENS // block_rows, dtype=jnp.int32))
    return blocks.reshape(TOKENS, HEADS * HEAD_DIM)

def mamba_layer(attended, segments, gate_input, state_proj, step_input, step_bias, decay_rate, skip_gain, conv_input, conv_state, norm_gain):
    positions = jnp.arange(TOKENS, dtype=jnp.int32)
    seg_tok = token_segments(segments, positions)
    rim_rows = CONV_TAPS - 1
    channels = SSM_HEADS * SSM_HEAD_DIM
    input_pad = jnp.concatenate([jnp.zeros((rim_rows, channels), jnp.bfloat16), attended]).astype(jnp.float32)
    state_pad = jnp.concatenate([jnp.zeros((rim_rows, 2, GROUPS, STATE), jnp.bfloat16), state_proj]).astype(jnp.float32)
    pos_pad = jnp.arange(-rim_rows, TOKENS, dtype=jnp.int32)
    seg_pad = token_segments(segments, pos_pad)
    input_conv = jnp.zeros((TOKENS, channels), jnp.float32)
    state_conv = jnp.zeros((TOKENS, 2, GROUPS, STATE), jnp.float32)
    for tap_id in range(CONV_TAPS):
        offset = rim_rows - tap_id
        same_doc = ((pos_pad[offset:offset + TOKENS] >= 0) & (seg_pad[offset:offset + TOKENS] == seg_tok)).astype(jnp.float32)
        input_conv = input_conv + conv_input[tap_id][None, :] * input_pad[offset:offset + TOKENS] * same_doc[:, None]
        state_conv = state_conv + conv_state[tap_id][None] * state_pad[offset:offset + TOKENS] * same_doc[:, None, None, None]
    input_conv = jax.nn.silu(input_conv)
    state_conv = jax.nn.silu(state_conv)
    step_dt = jax.nn.softplus(step_input + step_bias[None, :])
    prev_seg = jnp.concatenate([jnp.full((1,), -1, jnp.int32), seg_tok[:-1]])
    starts = (positions % BLOCK == 0) & (seg_tok != prev_seg)
    factor = jnp.where(starts[:, None], 0.0, jnp.exp(-step_dt * decay_rate[None, :]))
    per_group = SSM_HEADS // GROUPS
    input_heads = input_conv.reshape(TOKENS, SSM_HEADS, SSM_HEAD_DIM)

    def advance(carried, inputs):
        decay_now, dt_now, input_now, write_now, read_now = inputs
        write_heads = jnp.repeat(write_now, per_group, axis=0)
        read_heads = jnp.repeat(read_now, per_group, axis=0)
        carried = decay_now[:, None, None] * carried + (dt_now[:, None] * input_now)[:, :, None] * write_heads[:, None, :]
        return (carried, jnp.einsum('hn,hpn->hp', read_heads, carried, precision=full_prec))
    initial = jnp.zeros((SSM_HEADS, SSM_HEAD_DIM, STATE), jnp.float32)
    _, scan_out = lax.scan(advance, initial, (factor, step_dt, input_heads, state_conv[:, 0], state_conv[:, 1]))
    scan_out = scan_out + skip_gain[None, :, None] * input_heads
    gated_out = scan_out.reshape(TOKENS, channels) * jax.nn.silu(gate_input.astype(jnp.float32))
    mean_square = lax.optimization_barrier(jnp.mean(gated_out * gated_out, axis=1, keepdims=True))
    return (gated_out * norm_gain[None, :] / jnp.sqrt(mean_square + norm_eps)).astype(jnp.bfloat16)

def reference(queries, key_rows, value_rows, segments, gate_input, state_proj, step_input, step_bias, decay_rate, skip_gain, conv_input, conv_state, norm_gain):
    attention_out = attention_layer(queries, key_rows, value_rows, segments)
    mixer_out = mamba_layer(attention_out, segments, gate_input, state_proj, step_input, step_bias, decay_rate, skip_gain, conv_input, conv_state, norm_gain)
    return (attention_out, mixer_out)
```

```python
import functools
import math

import jax
import jax.numpy as jnp
from jax import lax
from jax.experimental import pallas as pl
from jax.experimental.pallas import tpu as pltpu
from jax.sharding import PartitionSpec as P

BLOCK = 128
NCTX = 32
NX = 4
NZ = 8
NTP = 8
ROWS = 512
HEADS = 8
HEAD_DIM = 128
SSM_HEADS = 16
SSM_DIM = 64
CHANNELS = 1024
STATE = 128
CHUNKS = ROWS // BLOCK
ALL_CHANNELS = 8192
NORM_EPS = 1e-05
EXP_SCALE = math.log2(math.e) / math.sqrt(HEAD_DIM)
HOPS = 6
FOLD_ORDER = (
    (1, 0), (0, 1), (2, 0), (0, 3), (0, 2),
    (1, 1), (3, 0), (1, 3), (1, 2),
    (2, 1), (4, 0), (2, 3), (2, 2),
    (3, 1), (3, 3), (3, 2),
    (4, 1), (4, 2),
)
Z_STEP = {1: 0, 2: 2, 3: 4, 4: 7, 5: 11}
X_STEP = {0: 0, 1: 1, 2: 5, 3: 9, 4: 13, 5: 16}
H_STEP = {0: 4, 1: 4, 2: 8, 3: 12, 4: 15, 5: 17}

f32 = jnp.float32
bf16 = jnp.bfloat16
HIGHEST = lax.Precision.HIGHEST


def dot(a, b, ca=1, cb=0, precision=None):
    return lax.dot_general(
        a, b, (((ca,), (cb,)), ((), ())), precision=precision, preferred_element_type=f32
    )


def remote(src, dst, send_sem, recv_sem, device):
    return pltpu.make_async_remote_copy(
        src_ref=src,
        dst_ref=dst,
        send_sem=send_sem,
        recv_sem=recv_sem,
        device_id=device,
        device_id_type=pl.DeviceIdType.MESH,
    )


def pick(table, n):
    value = jnp.int32(table[0])
    for i in range(1, len(table)):
        value = jnp.where(n >= i, jnp.int32(table[i]), value)
    return value


def attention_kernel(
    seg_ref, qt_ref, kv_ref, out_ref,
    slots, m_s, l_s, acc_s,
    send_z, send_p, send_m, send_a, send_b,
    recv_z, recv_p, recv_m, recv_a, recv_b,
):
    me = lax.axis_index("ctx")
    z, x = me // NX, me % NX
    up = {"ctx": lax.rem(z + 1, NZ) * NX + x}
    down = {"ctx": lax.rem(z + NZ - 1, NZ) * NX + x}
    right = {"ctx": z * NX + lax.rem(x + 1, NX)}
    left = {"ctx": z * NX + lax.rem(x + NX - 1, NX)}

    barrier = pltpu.get_barrier_semaphore()
    for peer in (up, down, right, left):
        pl.semaphore_signal(barrier, inc=1, device_id=peer, device_id_type=pl.DeviceIdType.MESH)
    pl.semaphore_wait(barrier, 4)

    half = kv_ref.shape[0] // 2

    def column(k):
        return kv_ref if k == 0 else slots.at[k, 0]

    def copy_z(k):
        return remote(column(k), slots.at[k + 1, 0], send_z.at[k], recv_z.at[k + 1], up)

    def copy_p(k):
        return remote(column(k), slots.at[k, 1], send_p.at[k], recv_p.at[k], right)

    def copy_m(k):
        return remote(column(k), slots.at[k, 3], send_m.at[k], recv_m.at[k], left)

    def copy_a(k):
        return remote(
            slots.at[k, 1, pl.ds(0, half)], slots.at[k, 2, pl.ds(0, half)],
            send_a.at[k], recv_a.at[k], right,
        )

    def copy_b(k):
        return remote(
            slots.at[k, 3, pl.ds(half, half)], slots.at[k, 2, pl.ds(half, half)],
            send_b.at[k], recv_b.at[k], left,
        )

    def z_step(k):
        if k > 0:
            copy_z(k - 1).wait_recv()
        if k < HOPS - 1:
            copy_z(k).start()
        copy_p(k).start()
        copy_m(k).start()

    def x_step(k):
        copy_p(k).wait_recv()
        copy_a(k).start()
        copy_m(k).wait_recv()
        copy_b(k).start()

    def h_step(k):
        copy_a(k).wait_recv()
        copy_b(k).wait_recv()

    z_step(0)

    def scores(k, qb, hp):
        return dot(k, qt_ref[qb, :, hp * 256 : (hp + 1) * 256])

    own_seg = [seg_ref[me * CHUNKS + c] for c in range(CHUNKS)]
    key_pos = lax.broadcasted_iota(jnp.int32, (BLOCK, 256), 0)
    query_pos = lax.broadcasted_iota(jnp.int32, (BLOCK, 256), 1) % BLOCK
    causal = key_pos <= query_pos
    tiles = [(qb, hp) for qb in range(CHUNKS) for hp in range(4)]

    def own_soft(qb, s):
        pens = [jnp.where(own_seg[b] == own_seg[qb], 0.0, 1e30).astype(f32) for b in range(qb)]
        last = jnp.where(causal, s[qb * BLOCK :], -1e30)
        m = jnp.max(last, axis=0, keepdims=True) * EXP_SCALE
        for b in range(qb):
            top = jnp.max(s[b * BLOCK : (b + 1) * BLOCK], axis=0, keepdims=True)
            m = jnp.maximum(m, top * EXP_SCALE - pens[b])
        total = jnp.zeros_like(m)
        parts = []
        for b in range(qb + 1):
            if b < qb:
                p = jnp.exp2(s[b * BLOCK : (b + 1) * BLOCK] * EXP_SCALE - (m + pens[b]))
            else:
                p = jnp.where(causal, jnp.exp2(last * EXP_SCALE - m), 0.0)
            total = total + jnp.sum(p, axis=0, keepdims=True)
            parts.append(p.astype(bf16))
        return m, total, jnp.concatenate(parts, axis=0)

    def values(block, count):
        return jnp.concatenate(
            [block[half + b * BLOCK : half + (b + 1) * BLOCK] for b in range(count)], axis=1
        )

    def own_fold(t, m, total, p):
        qb, hp = t
        i = qb * 4 + hp
        m_s[i] = m
        l_s[i] = total
        acc_s[i] = dot(values(kv_ref, qb + 1), p)

    s_now = scores(kv_ref[0:BLOCK], 0, 0)
    waiting = None
    for n, t in enumerate(tiles):
        s_next = None
        if n + 1 < len(tiles):
            qb, hp = tiles[n + 1]
            s_next = scores(kv_ref[0 : (qb + 1) * BLOCK], qb, hp)
        done = own_soft(t[0], s_now)
        if waiting is not None:
            own_fold(waiting[0], *waiting[1])
        waiting = (t, done)
        s_now = s_next
    own_fold(waiting[0], *waiting[1])

    def soft(i, s, pens):
        m = m_s[i]
        new = m
        for b in range(CHUNKS):
            top = jnp.max(s[b * BLOCK : (b + 1) * BLOCK], axis=0, keepdims=True)
            new = jnp.maximum(new, top * EXP_SCALE - pens[b])
        total = jnp.zeros_like(m)
        parts = []
        for b in range(CHUNKS):
            p = jnp.exp2(s[b * BLOCK : (b + 1) * BLOCK] * EXP_SCALE - (new + pens[b]))
            total = total + jnp.sum(p, axis=0, keepdims=True)
            parts.append(p.astype(bf16))
        shrink = jnp.exp2(m - new)
        m_s[i] = new
        l_s[i] = l_s[i] * shrink + total
        return shrink, jnp.concatenate(parts, axis=0)

    def fold_block(n, carry):
        for k in range(HOPS):
            if k in Z_STEP:
                pl.when(n == Z_STEP[k])(functools.partial(z_step, k))
            pl.when(n == X_STEP[k])(functools.partial(x_step, k))
        for k in range(HOPS):
            pl.when(n == H_STEP[k])(functools.partial(h_step, k))
        rank = pick([o[0] for o in FOLD_ORDER], n)
        col = pick([o[1] for o in FOLD_ORDER], n)
        source = me - (NX * rank + col)
        k = jnp.where(x >= col, rank, rank + 1)
        first = jnp.maximum(source, 0) * CHUNKS
        key_seg = [seg_ref[first + b] for b in range(CHUNKS)]
        pens = [
            [
                jnp.where((source >= 0) & (key_seg[b] == own_seg[qb]), 0.0, 1e30).astype(f32)
                for b in range(CHUNKS)
            ]
            for qb in range(CHUNKS)
        ]
        keys = slots[k, col, 0:half]
        vt = jnp.concatenate(
            [slots[k, col, half + b * BLOCK : half + (b + 1) * BLOCK] for b in range(CHUNKS)],
            axis=1,
        )

        def fold(t, shrink, p):
            i = t[0] * 4 + t[1]
            acc_s[i] = acc_s[i] * shrink + dot(vt, p)

        s_now = scores(keys, 0, 0)
        waiting = None
        for n_tile, t in enumerate(tiles):
            s_next = scores(keys, *tiles[n_tile + 1]) if n_tile + 1 < len(tiles) else None
            done = soft(t[0] * 4 + t[1], s_now, pens[t[0]])
            if waiting is not None:
                fold(waiting[0], *waiting[1])
            waiting = (t, done)
            s_now = s_next
        fold(waiting[0], *waiting[1])
        return carry

    lax.fori_loop(0, len(FOLD_ORDER), fold_block, 0)

    for qb, hp in tiles:
        i = qb * 4 + hp
        o = acc_s[i] / l_s[i]
        for j in range(2):
            c = (hp * 2 + j) * HEAD_DIM
            part = o[:, j * BLOCK : (j + 1) * BLOCK].T
            out_ref[qb * BLOCK : (qb + 1) * BLOCK, c : c + HEAD_DIM] = part.astype(bf16)

    for k in range(HOPS):
        if k < HOPS - 1:
            copy_z(k).wait_send()
        copy_p(k).wait_send()
        copy_m(k).wait_send()
        copy_a(k).wait_send()
        copy_b(k).wait_send()


def attention(segments, qt, kv):
    dma = pltpu.SemaphoreType.DMA
    return pl.pallas_call(
        attention_kernel,
        out_shape=jax.ShapeDtypeStruct((ROWS, CHANNELS), bf16),
        in_specs=[
            pl.BlockSpec(memory_space=pltpu.SMEM),
            pl.BlockSpec(memory_space=pltpu.VMEM),
            pl.BlockSpec(memory_space=pltpu.VMEM),
        ],
        out_specs=pl.BlockSpec(memory_space=pltpu.VMEM),
        scratch_shapes=[
            pltpu.VMEM((HOPS, NX, 2 * ROWS, HEAD_DIM), bf16),
            pltpu.VMEM((16, 1, 256), f32),
            pltpu.VMEM((16, 1, 256), f32),
            pltpu.VMEM((16, HEAD_DIM, 256), f32),
        ]
        + [dma((HOPS,))] * 10,
        compiler_params=pltpu.CompilerParams(
            collective_id=0, has_side_effects=True, vmem_limit_bytes=56 << 20
        ),
        cost_estimate=pl.CostEstimate(
            flops=20 * 10**9, bytes_accessed=4 << 20, transcendentals=40 * 10**6
        ),
        name="attention",
    )(segments, qt, kv)


def silu(v):
    return v / (1.0 + jnp.exp(-v))


def softplus(v):
    return jnp.maximum(v, 0.0) + jnp.log1p(jnp.exp(-jnp.abs(v)))


def split(v):
    high = v.astype(bf16)
    return high, (v - high.astype(f32)).astype(bf16)


def spread(v, expand):
    high, low = split(v)
    return dot(high, expand) + dot(low, expand)


def mixer_kernel(
    seg_ref, att_ref, gate_ref, proj_ref, step_ref, step_t_ref, bias_ref, bias_t_ref,
    rate_ref, rate_t_ref, skip_ref, tap_ref, tap_state_ref, gain_ref, out_ref,
    halo_a, halo_s, ext, ext_s, xs, cs, ys, gs, enter,
    t_send, t_all, s_send, s_in, p_send, p_in, q_all,
    halo_sems, t_sems, s_sems, p_sems, q_sems,
    halo_recv, t_recv, s_recv, p_recv, q_recv,
):
    me = lax.axis_index("ctx")
    tp = lax.axis_index("tp")
    mesh_id = pl.DeviceIdType.MESH
    barrier = pltpu.get_barrier_semaphore()

    def greet_ctx(o, c):
        pl.semaphore_signal(
            barrier, inc=1, device_id={"ctx": lax.rem(me + o, NCTX)}, device_id_type=mesh_id
        )
        return c

    def greet_tp(o, c):
        pl.semaphore_signal(
            barrier, inc=1, device_id={"tp": lax.rem(tp + o, NTP)}, device_id_type=mesh_id
        )
        return c

    lax.fori_loop(1, NCTX, greet_ctx, 0)
    lax.fori_loop(1, NTP, greet_tp, 0)

    iota_r = lax.broadcasted_iota(jnp.int32, (BLOCK, BLOCK), 0)
    iota_c = lax.broadcasted_iota(jnp.int32, (BLOCK, BLOCK), 1)
    lower = iota_r >= iota_c
    tri = jnp.where(lower, 1.0, 0.0).astype(f32)
    expand = jnp.where(
        lax.broadcasted_iota(jnp.int32, (SSM_HEADS, CHANNELS), 1) // SSM_DIM
        == lax.broadcasted_iota(jnp.int32, (SSM_HEADS, CHANNELS), 0),
        1.0,
        0.0,
    ).astype(bf16)
    keep = []
    for c in range(CHUNKS):
        at = me * CHUNKS + c
        same = (at > 0) & (seg_ref[at] == seg_ref[jnp.maximum(at - 1, 0)])
        keep.append(jnp.where(same, 1.0, 0.0).astype(f32))
    dt, dt_t, cum, cum_t = [], [], [], []
    for c in range(CHUNKS):
        rows = slice(c * BLOCK, (c + 1) * BLOCK)
        d = softplus(step_ref[rows, :] + bias_ref[...])
        d_t = softplus(step_t_ref[:, rows] + bias_t_ref[...])
        dt.append(d)
        dt_t.append(d_t)
        cum.append(dot(tri, -d * rate_ref[...], precision=HIGHEST))
        cum_t.append(dot(-d_t * rate_t_ref[...], tri, 1, 1, precision=HIGHEST))
    last = [v[BLOCK - 1 : BLOCK, :] for v in cum]
    factor = [keep[c] * jnp.exp(last[c]) for c in range(CHUNKS)]
    prefix = [jnp.ones_like(last[0])]
    for c in range(CHUNKS):
        prefix.append(prefix[-1] * factor[c])
    t_send[...] = jnp.zeros_like(t_send)
    t_send[0:1, 0:SSM_HEADS] = prefix[CHUNKS]

    pl.semaphore_wait(barrier, NCTX - 1 + NTP - 1)

    tail = ROWS - 16
    following = {"ctx": lax.rem(me + 1, NCTX)}
    send_att = remote(
        att_ref.at[pl.ds(tail, 16)], halo_a, halo_sems.at[0], halo_recv.at[0], following
    )
    send_proj = remote(
        proj_ref.at[pl.ds(tail, 16)], halo_s, halo_sems.at[1], halo_recv.at[1], following
    )
    send_att.start()
    send_proj.start()

    def t_copy(o, slot):
        return remote(
            t_send, t_all.at[slot], t_sems.at[o], t_recv.at[slot], {"ctx": lax.rem(me + o, NCTX)}
        )

    def s_copy(o, slot):
        to = lax.rem(me + o, NCTX)
        return remote(s_send.at[to], s_in.at[slot], s_sems.at[o], s_recv.at[slot], {"ctx": to})

    def p_copy(o, slot):
        to = lax.rem(me + o, NCTX)
        return remote(p_send.at[to], p_in.at[slot], p_sems.at[o], p_recv.at[slot], {"ctx": to})

    def q_copy(o, slot):
        return remote(
            q_all.at[tp], q_all.at[slot], q_sems.at[o], q_recv.at[slot],
            {"tp": lax.rem(tp + o, NTP)},
        )

    def start_all(copy, count, place):
        def one(o, c):
            copy(o, place).start()
            return c

        lax.fori_loop(1, count, one, 0)

    def recv_all(copy, count, place):
        def one(o, c):
            copy(o, lax.rem(place + o, count)).wait_recv()
            return c

        lax.fori_loop(1, count, one, 0)

    def sent_all(copy, count, place):
        def one(o, c):
            copy(o, place).wait_send()
            return c

        lax.fori_loop(1, count, one, 0)

    start_all(t_copy, NCTX, me)
    t_all[me] = t_send[...]

    send_att.wait_recv()
    send_proj.wait_recv()

    state = jnp.zeros((STATE, CHANNELS), f32)
    for c in range(CHUNKS):
        rows = slice(c * BLOCK, (c + 1) * BLOCK)
        if c == 0:
            ext[0:8] = halo_a[...].astype(f32)[8:16] * keep[c]
            ext_s[0:8] = halo_s[...].astype(f32)[8:16] * keep[c]
        else:
            before = slice(c * BLOCK - 16, c * BLOCK)
            ext[0:8] = att_ref[before, :].astype(f32)[8:16] * keep[c]
            ext_s[0:8] = proj_ref[before, :].astype(f32)[8:16] * keep[c]
        ext[8:] = att_ref[rows, :].astype(f32)
        ext_s[8:] = proj_ref[rows, :].astype(f32)
        conv = tap_ref[0:1, :] * ext[8 : 8 + BLOCK]
        conv_s = tap_state_ref[0:1, :] * ext_s[8 : 8 + BLOCK]
        for k in range(1, 4):
            conv = conv + tap_ref[k : k + 1, :] * ext[8 - k : 8 - k + BLOCK]
            conv_s = conv_s + tap_state_ref[k : k + 1, :] * ext_s[8 - k : 8 - k + BLOCK]
        conv = silu(conv)
        conv_s = silu(conv_s)
        xs[rows, :] = conv
        cs[rows, :] = conv_s
        enter[c] = state.astype(bf16)
        to_end = jnp.exp(last[c] - cum[c]) * dt[c]
        scaled = (conv * spread(to_end, expand)).astype(bf16)
        write_t = conv_s[:, 0:STATE].T.astype(bf16)
        pair = jnp.concatenate([factor[c], jnp.zeros((7, SSM_HEADS), f32)], axis=0)
        state = state * spread(pair, expand)[0:1] + dot(write_t, scaled)

    for ng in range(8):
        for cg in range(4):
            s_send[ng * 4 + cg] = state[
                ng * 16 : (ng + 1) * 16, cg * 256 : (cg + 1) * 256
            ].astype(bf16)
    start_all(s_copy, NCTX, me)
    s_in[me] = s_send[me]

    low_half = lax.broadcasted_iota(jnp.int32, (BLOCK, BLOCK), 1) < SSM_DIM
    for c in range(CHUNKS):
        rows = slice(c * BLOCK, (c + 1) * BLOCK)
        write = cs[rows, 0:STATE]
        read = cs[rows, STATE:]
        meet = dot(read, write, 1, 1, precision=HIGHEST)
        conv = xs[rows, :]
        begin = spread(jnp.exp(cum[c]) * keep[c], expand)
        out = dot(read.astype(bf16), enter[c]) * begin + conv * skip_ref[...]
        parts = []
        for pair in range(SSM_HEADS // 2):
            mixes = []
            for h in (2 * pair, 2 * pair + 1):
                gap = cum[c][:, h : h + 1] - cum_t[c][h : h + 1, :]
                mix = jnp.exp(jnp.where(lower, gap, 0.0)) * meet * dt_t[c][h : h + 1, :]
                mixes.append(jnp.where(lower, mix, 0.0).astype(bf16))
            both = conv[:, pair * BLOCK : (pair + 1) * BLOCK]
            stacked = jnp.concatenate(
                [jnp.where(low_half, both, 0.0), jnp.where(low_half, 0.0, both)], axis=0
            ).astype(bf16)
            parts.append(dot(jnp.concatenate(mixes, axis=1), stacked))
        ys[rows, :] = out + jnp.concatenate(parts, axis=1)

    recv_all(t_copy, NCTX, me)
    share = lax.rem(me, 4)
    expand_share = jnp.where(
        lax.broadcasted_iota(jnp.int32, (BLOCK, 256), 1) // SSM_DIM + share * 4
        == lax.broadcasted_iota(jnp.int32, (BLOCK, 256), 0),
        1.0,
        0.0,
    ).astype(bf16)
    decays = spread(t_all[:, 0, :], expand_share)
    recv_all(s_copy, NCTX, me)
    running = jnp.zeros((16, 256), f32)
    for d in range(NCTX):
        p_send[d] = running.astype(bf16)
        running = running * decays[d : d + 1, :] + s_in[d].astype(f32)
    start_all(p_copy, NCTX, me)
    p_in[me] = p_send[me]

    for c in range(CHUNKS):
        rows = slice(c * BLOCK, (c + 1) * BLOCK)
        gs[rows, :] = silu(gate_ref[rows, :].astype(f32))

    recv_all(p_copy, NCTX, me)
    incoming = jnp.concatenate(
        [
            jnp.concatenate([p_in[ng * 4 + cg] for cg in range(4)], axis=1)
            for ng in range(8)
        ],
        axis=0,
    )
    squares = []
    for c in range(CHUNKS):
        rows = slice(c * BLOCK, (c + 1) * BLOCK)
        begin = spread(jnp.exp(cum[c]) * (prefix[c] * keep[c]), expand)
        out = ys[rows, :] + dot(cs[rows, STATE:].astype(bf16), incoming) * begin
        gated = out * gs[rows, :]
        gs[rows, :] = gated
        sq = gated * gated
        folded = sq[:, 0:BLOCK]
        for i in range(1, CHANNELS // BLOCK):
            folded = folded + sq[:, i * BLOCK : (i + 1) * BLOCK]
        squares.append(jnp.sum(folded.T, axis=0, keepdims=True))
    squares.append(jnp.zeros((8 - CHUNKS, BLOCK), f32))
    q_all[tp] = jnp.concatenate(squares, axis=0)
    start_all(q_copy, NTP, tp)
    recv_all(q_copy, NTP, tp)
    total = q_all[0]
    for i in range(1, NTP):
        total = total + q_all[i]
    scale = lax.rsqrt(total * (1.0 / ALL_CHANNELS) + NORM_EPS)
    for c in range(CHUNKS):
        rows = slice(c * BLOCK, (c + 1) * BLOCK)
        by_row = jnp.broadcast_to(scale[c : c + 1, :], (BLOCK, BLOCK)).T
        for i in range(CHANNELS // BLOCK):
            cols = slice(i * BLOCK, (i + 1) * BLOCK)
            out_ref[rows, cols] = (gs[rows, cols] * gain_ref[:, cols] * by_row).astype(bf16)

    send_att.wait_send()
    send_proj.wait_send()
    sent_all(t_copy, NCTX, me)
    sent_all(s_copy, NCTX, me)
    sent_all(p_copy, NCTX, me)
    sent_all(q_copy, NTP, tp)


def mixer(segments, *arrays):
    dma = pltpu.SemaphoreType.DMA
    vmem = pltpu.VMEM
    return pl.pallas_call(
        mixer_kernel,
        out_shape=jax.ShapeDtypeStruct((ROWS, CHANNELS), bf16),
        in_specs=[pl.BlockSpec(memory_space=pltpu.SMEM)]
        + [pl.BlockSpec(memory_space=pltpu.VMEM)] * len(arrays),
        out_specs=pl.BlockSpec(memory_space=pltpu.VMEM),
        scratch_shapes=[
            vmem((16, CHANNELS), bf16),
            vmem((16, 2 * STATE), bf16),
            vmem((8 + BLOCK, CHANNELS), f32),
            vmem((8 + BLOCK, 2 * STATE), f32),
            vmem((ROWS, CHANNELS), f32),
            vmem((ROWS, 2 * STATE), f32),
            vmem((ROWS, CHANNELS), f32),
            vmem((ROWS, CHANNELS), f32),
            vmem((CHUNKS, STATE, CHANNELS), bf16),
            vmem((8, BLOCK), f32),
            vmem((NCTX, 8, BLOCK), f32),
            vmem((NCTX, 16, 256), bf16),
            vmem((NCTX, 16, 256), bf16),
            vmem((NCTX, 16, 256), bf16),
            vmem((NCTX, 16, 256), bf16),
            vmem((NTP, 8, BLOCK), f32),
            dma((2,)), dma((NCTX,)), dma((NCTX,)), dma((NCTX,)), dma((NTP,)),
            dma((2,)), dma((NCTX,)), dma((NCTX,)), dma((NCTX,)), dma((NTP,)),
        ],
        compiler_params=pltpu.CompilerParams(
            collective_id=1, has_side_effects=True, vmem_limit_bytes=56 << 20
        ),
        cost_estimate=pl.CostEstimate(
            flops=2 * 10**9, bytes_accessed=6 << 20, transcendentals=3 * 10**6
        ),
        name="mixer",
    )(segments, *arrays)


def local(
    queries, key_rows, value_rows, segments, gate_input, state_proj, step_input, step_bias,
    decay_rate, skip_gain, conv_input, conv_state, norm_gain,
):
    qt = queries.reshape(CHUNKS, BLOCK, HEADS, HEAD_DIM).transpose(0, 3, 2, 1)
    qt = qt.reshape(CHUNKS, HEAD_DIM, HEADS * BLOCK)
    vt = value_rows.reshape(CHUNKS, BLOCK, HEAD_DIM).transpose(0, 2, 1)
    kv = jnp.concatenate([key_rows.reshape(ROWS, HEAD_DIM), vt.reshape(ROWS, HEAD_DIM)])
    attended = attention(segments, qt, kv)
    mixer_out = mixer(
        segments,
        attended,
        gate_input,
        state_proj.reshape(ROWS, 2 * STATE),
        step_input,
        step_input.T,
        step_bias[None, :],
        step_bias[:, None],
        decay_rate[None, :],
        decay_rate[:, None],
        jnp.repeat(skip_gain, SSM_DIM)[None, :],
        conv_input,
        conv_state.reshape(4, 2 * STATE),
        norm_gain[None, :],
    )
    return attended, mixer_out


def solution(mesh):
    placed = (
        P("ctx", "tp", None),
        P("ctx", "tp", None),
        P("ctx", "tp", None),
        P(),
        P("ctx", "tp"),
        P("ctx", None, "tp", None),
        P("ctx", "tp"),
        P("tp"),
        P("tp"),
        P("tp"),
        P(None, "tp"),
        P(None, None, "tp", None),
        P("tp"),
    )
    return jax.shard_map(
        local,
        mesh=mesh,
        in_specs=placed,
        out_specs=(P("ctx", "tp"), P("ctx", "tp")),
        check_vma=False,
    )
```

```python
import functools
import math

import jax
import jax.numpy as jnp
from jax import lax
from jax.experimental import pallas as pl
from jax.experimental.pallas import tpu as pltpu
from jax.sharding import PartitionSpec as P

BLOCK = 128
NCTX = 32
NX = 4
NZ = 8
NTP = 8
ROWS = 512
HEADS = 8
HEAD_DIM = 128
SSM_HEADS = 16
SSM_DIM = 64
CHANNELS = 1024
STATE = 128
CHUNKS = ROWS // BLOCK
ALL_CHANNELS = 8192
NORM_EPS = 1e-05
EXP_SCALE = math.log2(math.e) / math.sqrt(HEAD_DIM)
HOPS = 6
FOLD_ORDER = (
    (1, 0), (2, 0), (0, 1), (0, 3), (0, 2), (1, 1), (3, 0), (1, 3), (1, 2),
    (2, 1), (4, 0), (2, 3), (2, 2), (3, 1), (3, 3), (3, 2), (4, 1), (4, 2),
)
STEPS = (
    (),
    (("z", 3), ("h", 0), ("h", 1)),
    (("x", 2),),
    (("z", 4),),
    (("h", 2), ("x", 3)),
    (("x", 4),),
    (("h", 3), ("h", 4)),
    (),
    (("x", 5), ("h", 5)),
)

f32 = jnp.float32
bf16 = jnp.bfloat16
HIGHEST = lax.Precision.HIGHEST
MESH_ID = pl.DeviceIdType.MESH


def dot(a, b, ca=1, cb=0, precision=None):
    return lax.dot_general(
        a, b, (((ca,), (cb,)), ((), ())), precision=precision, preferred_element_type=f32
    )


def remote(src, dst, send_sem, recv_sem, device):
    return pltpu.make_async_remote_copy(
        src_ref=src,
        dst_ref=dst,
        send_sem=send_sem,
        recv_sem=recv_sem,
        device_id=device,
        device_id_type=MESH_ID,
    )


def pick(table, n):
    value = jnp.int32(table[0])
    for i in range(1, len(table)):
        value = jnp.where(n >= i, jnp.int32(table[i]), value)
    return value


def silu(v):
    return v / (1.0 + jnp.exp(-v))


def softplus(v):
    return jnp.maximum(v, 0.0) + jnp.log1p(jnp.exp(-jnp.abs(v)))


def split(v):
    high = v.astype(bf16)
    return high, (v - high.astype(f32)).astype(bf16)


def spread(v, expand):
    high, low = split(v)
    return dot(high, expand) + dot(low, expand)


def chunk(c):
    return slice(c * BLOCK, (c + 1) * BLOCK)


def layer_kernel(
    seg_ref, q_ref, k_ref, v_ref, gate_ref, proj_ref, step_ref, bias_ref, rate_ref, skip_ref,
    tap_ref, tap_state_ref, gain_ref, att_ref, out_ref,
    wide, qt, kv, slots, m_s, l_s, acc_s,
    halo_a, halo_s, tail_a, tail_s, ext, ext_s, xs, cs, gs, mix_s, frag, heads_s, row_s,
    t_send, t_all, s_send, s_in, p_send, p_in, q_all,
    send_z, send_p, send_m, send_a, send_b, send_c,
    recv_z, recv_p, recv_m, recv_a, recv_b, recv_c,
    halo_sems, t_sems, s_sems, p_sems, q_sems,
    halo_recv, t_recv, s_recv, p_recv, q_recv,
):
    me = lax.axis_index("ctx")
    tp = lax.axis_index("tp")
    z, x = me // NX, me % NX
    up = {"ctx": lax.rem(z + 1, NZ) * NX + x}
    right = {"ctx": z * NX + lax.rem(x + 1, NX)}
    left = {"ctx": z * NX + lax.rem(x + NX - 1, NX)}

    barrier = pltpu.get_barrier_semaphore()

    def greet_ctx(o, c):
        pl.semaphore_signal(
            barrier, inc=1, device_id={"ctx": lax.rem(me + o, NCTX)}, device_id_type=MESH_ID
        )
        return c

    def greet_tp(o, c):
        pl.semaphore_signal(
            barrier, inc=1, device_id={"tp": lax.rem(tp + o, NTP)}, device_id_type=MESH_ID
        )
        return c

    lax.fori_loop(1, NCTX, greet_ctx, 0)
    lax.fori_loop(1, NTP, greet_tp, 0)

    half = ROWS
    kv[0:half] = k_ref[...]
    for c in range(CHUNKS):
        kv[half + c * BLOCK : half + (c + 1) * BLOCK] = (
            v_ref[chunk(c), :].astype(f32).T.astype(bf16)
        )
    tail_s[...] = proj_ref[2 * ROWS - 32 :, :]

    pl.semaphore_wait(barrier, NCTX - 1 + NTP - 1)

    def copy_z(k):
        return remote(
            kv if k == 0 else slots.at[k, 0], slots.at[k + 1, 0], send_z.at[k], recv_z.at[k + 1], up
        )

    def copy_p(k):
        return remote(
            kv if k == 0 else slots.at[k, 0], slots.at[k, 1], send_p.at[k], recv_p.at[k], right
        )

    def copy_m(k):
        return remote(
            kv if k == 0 else slots.at[k, 0], slots.at[k, 3], send_m.at[k], recv_m.at[k], left
        )

    def copy_a(k):
        rows = pl.ds(0, 2 * half if k == 0 else half)
        return remote(
            slots.at[k, 1, rows], slots.at[k, 2, rows], send_a.at[k], recv_a.at[k], right
        )

    def copy_b(k):
        rows = pl.ds(half, half)
        return remote(
            slots.at[k, 3, rows], slots.at[k, 2, rows], send_b.at[k], recv_b.at[k], left
        )

    def copy_c(k):
        return remote(
            slots.at[k - 1, 2], slots.at[k, 2], send_c.at[k], recv_c.at[k], up
        )

    def copy_d(k):
        return remote(
            slots.at[k - 1, 1], slots.at[k, 1], send_p.at[k], recv_p.at[k], up
        )

    top = HOPS - 1
    through_z = (2,)
    always = None
    moves = {("z", k): (copy_z, always, always) for k in range(top - 1)}
    for k in range(1, top):
        moves["p", k] = (copy_p, always, always)
        moves["m", k] = (copy_m, always, always)
        if k in through_z:
            moves["c", k] = (copy_c, always, always)
        else:
            moves["a", k] = (copy_a, always, always)
            moves["b", k] = (copy_b, always, always)
    moves["p", 0] = (copy_p, x < 3, x >= 1)
    moves["m", 0] = (copy_m, x == 0, x == 3)
    moves["a", 0] = (copy_a, (x == 1) | (x == 2), x >= 2)
    moves["d", top] = (copy_d, x == 0, x == 0)
    moves["c", top] = (copy_c, x <= 1, x <= 1)

    def act(kind, k, what):
        if (kind, k) not in moves:
            return
        make, sends, receives = moves[kind, k]
        condition = receives if what == "wait_recv" else sends

        def do():
            getattr(make(k), what)()

        if condition is None:
            do()
        else:
            pl.when(condition)(do)

    def z_step(k):
        if k > 0:
            act("z", k - 1, "wait_recv")
        for kind in ("z", "p", "m"):
            act(kind, k, "start")

    def x_step(k):
        act("p", k, "wait_recv")
        act("a", k, "start")
        act("m", k, "wait_recv")
        act("b", k, "start")
        act("d", k, "wait_recv")
        act("d", k + 1, "start")

    def h_step(k):
        for kind in ("a", "b", "c"):
            act(kind, k, "wait_recv")
        act("c", k + 1, "start")

    z_step(0)

    following = {"ctx": lax.rem(me + 1, NCTX)}
    send_proj = remote(tail_s, halo_s, halo_sems.at[1], halo_recv.at[1], following)
    send_proj.start()

    def t_copy(o, slot):
        return remote(
            t_send, t_all.at[slot], t_sems.at[o], t_recv.at[slot], {"ctx": lax.rem(me + o, NCTX)}
        )

    def s_copy(o, slot):
        to = lax.rem(me + o, NCTX)
        return remote(s_send.at[to], s_in.at[slot], s_sems.at[o], s_recv.at[slot], {"ctx": to})

    def p_copy(o, slot):
        to = lax.rem(me + o, NCTX)
        return remote(p_send.at[to], p_in.at[slot], p_sems.at[o], p_recv.at[slot], {"ctx": to})

    def q_copy(o, slot):
        return remote(
            q_all.at[tp], q_all.at[slot], q_sems.at[o], q_recv.at[slot],
            {"tp": lax.rem(tp + o, NTP)},
        )

    def start_all(copy, count, place):
        def one(o, c):
            copy(o, place).start()
            return c

        lax.fori_loop(1, count, one, 0)

    def recv_all(copy, count, place):
        def one(o, c):
            copy(o, lax.rem(place + o, count)).wait_recv()
            return c

        lax.fori_loop(1, count, one, 0)

    def sent_all(copy, count, place):
        def one(o, c):
            copy(o, place).wait_send()
            return c

        lax.fori_loop(1, count, one, 0)

    wide[...] = q_ref[...].astype(f32)
    for qb in range(CHUNKS):
        for h in range(HEADS):
            part = wide[pl.ds(qb * BLOCK * HEADS + h, BLOCK, stride=HEADS), :]
            qt[qb, :, h * BLOCK : (h + 1) * BLOCK] = part.T.astype(bf16)

    def scores(keys, qb, hp):
        return dot(keys, qt[qb, :, hp * 256 : (hp + 1) * 256])

    own_seg = [seg_ref[me * CHUNKS + c] for c in range(CHUNKS)]
    key_pos = lax.broadcasted_iota(jnp.int32, (BLOCK, 256), 0)
    query_pos = lax.broadcasted_iota(jnp.int32, (BLOCK, 256), 1) % BLOCK
    causal = key_pos <= query_pos
    tiles = [(qb, hp) for qb in range(CHUNKS) for hp in range(4)]

    def own_soft(qb, s):
        pens = [jnp.where(own_seg[b] == own_seg[qb], 0.0, 1e30).astype(f32) for b in range(qb)]
        last = jnp.where(causal, s[qb * BLOCK :], -1e30)
        m = jnp.max(last, axis=0, keepdims=True) * EXP_SCALE
        for b in range(qb):
            most = jnp.max(s[b * BLOCK : (b + 1) * BLOCK], axis=0, keepdims=True)
            m = jnp.maximum(m, most * EXP_SCALE - pens[b])
        total = jnp.zeros_like(m)
        parts = []
        for b in range(qb + 1):
            if b < qb:
                p = jnp.exp2(s[b * BLOCK : (b + 1) * BLOCK] * EXP_SCALE - (m + pens[b]))
            else:
                p = jnp.where(causal, jnp.exp2(last * EXP_SCALE - m), 0.0)
            total = total + jnp.sum(p, axis=0, keepdims=True)
            parts.append(p.astype(bf16))
        return m, total, jnp.concatenate(parts, axis=0)

    def values(block, count):
        return jnp.concatenate(
            [block[half + b * BLOCK : half + (b + 1) * BLOCK] for b in range(count)], axis=1
        )

    def own_fold(t, m, total, p):
        qb, hp = t
        i = qb * 4 + hp
        m_s[i] = m
        l_s[i] = total
        acc_s[i] = dot(values(kv, qb + 1), p)

    s_now = scores(kv[0:BLOCK], 0, 0)
    waiting = None
    for n, t in enumerate(tiles):
        s_next = None
        if n + 1 < len(tiles):
            qb, hp = tiles[n + 1]
            s_next = scores(kv[0 : (qb + 1) * BLOCK], qb, hp)
        done = own_soft(t[0], s_now)
        if waiting is not None:
            own_fold(waiting[0], *waiting[1])
        waiting = (t, done)
        s_now = s_next
    own_fold(waiting[0], *waiting[1])

    iota_r = lax.broadcasted_iota(jnp.int32, (BLOCK, BLOCK), 0)
    iota_c = lax.broadcasted_iota(jnp.int32, (BLOCK, BLOCK), 1)
    lower = iota_r >= iota_c
    tri = jnp.where(lower, 1.0, 0.0).astype(f32)
    expand = jnp.where(
        lax.broadcasted_iota(jnp.int32, (SSM_HEADS, CHANNELS), 1) // SSM_DIM
        == lax.broadcasted_iota(jnp.int32, (SSM_HEADS, CHANNELS), 0),
        1.0,
        0.0,
    ).astype(bf16)
    diagonal = lax.broadcasted_iota(jnp.int32, (SSM_HEADS, SSM_HEADS), 0) == (
        lax.broadcasted_iota(jnp.int32, (SSM_HEADS, SSM_HEADS), 1)
    )

    def as_column(row):
        square = jnp.broadcast_to(row, (SSM_HEADS, SSM_HEADS))
        return jnp.sum(jnp.where(diagonal, square, 0.0), axis=1, keepdims=True)

    bias = as_column(bias_ref[...])
    rate = as_column(rate_ref[...])
    keep = []
    for c in range(CHUNKS):
        at = me * CHUNKS + c
        same = (at > 0) & (seg_ref[at] == seg_ref[jnp.maximum(at - 1, 0)])
        keep.append(jnp.where(same, 1.0, 0.0).astype(f32))
    dt_t = [softplus(step_ref[:, chunk(c)] + bias) for c in range(CHUNKS)]
    cum_t = [dot(-dt_t[c] * rate, tri, 1, 1, precision=HIGHEST) for c in range(CHUNKS)]
    cum = [v.T for v in cum_t]
    last = [v[BLOCK - 1 : BLOCK, :] for v in cum]
    factor = [keep[c] * jnp.exp(last[c]) for c in range(CHUNKS)]
    prefix = [jnp.ones_like(last[0])]
    for c in range(CHUNKS):
        prefix.append(prefix[-1] * factor[c])
    t_send[...] = jnp.zeros_like(t_send)
    t_send[0:1, 0:SSM_HEADS] = prefix[CHUNKS]
    start_all(t_copy, NCTX, me)
    t_all[me] = t_send[...]
    for c in range(CHUNKS):
        begin = jnp.exp(cum[c]) * keep[c]
        heads_s[0, chunk(c), :] = jnp.exp(last[c] - cum[c]) * dt_t[c].T
        heads_s[1, chunk(c), :] = begin
        heads_s[2, chunk(c), :] = begin * prefix[c]
    rows = factor + [skip_ref[...]]
    rows = jnp.concatenate(rows + [jnp.zeros((8 - len(rows), SSM_HEADS), f32)], axis=0)
    row_s[...] = spread(rows, expand)

    z_step(1)

    send_proj.wait_recv()
    wide[0 : 2 * ROWS, :] = proj_ref[...].astype(f32)
    wide[2 * ROWS : 2 * ROWS + 32, :] = halo_s[...].astype(f32)
    for c in range(CHUNKS):
        for r in range(2):
            cols = slice(r * STATE, (r + 1) * STATE)
            first = 2 * ROWS + 16 if c == 0 else 2 * (c * BLOCK - 8)
            ext_s[0:8, cols] = wide[pl.ds(first + r, 8, stride=2), :] * keep[c]
            ext_s[8:, cols] = wide[pl.ds(2 * c * BLOCK + r, BLOCK, stride=2), :]
            conv = tap_state_ref[r : r + 1, :] * ext_s[8 : 8 + BLOCK, cols]
            for k in range(1, 4):
                tap = tap_state_ref[2 * k + r : 2 * k + r + 1, :]
                conv = conv + tap * ext_s[8 - k : 8 - k + BLOCK, cols]
            cs[chunk(c), cols] = silu(conv)
        meet = dot(cs[chunk(c), STATE:], cs[chunk(c), 0:STATE], 1, 1, precision=HIGHEST)
        for h in range(SSM_HEADS):
            gap = cum[c][:, h : h + 1] - cum_t[c][h : h + 1, :]
            mix = jnp.exp(jnp.where(lower, gap, 0.0)) * meet * dt_t[c][h : h + 1, :]
            mix_s[c, h // 2, :, (h % 2) * BLOCK : (h % 2 + 1) * BLOCK] = jnp.where(
                lower, mix, 0.0
            ).astype(bf16)
        gs[chunk(c), :] = silu(gate_ref[chunk(c), :].astype(f32))
        if c == CHUNKS - 2:
            x_step(0)
            x_step(1)
            z_step(2)

    def soft(i, s, pens):
        m = m_s[i]
        new = m
        for b, pen in enumerate(pens):
            most = jnp.max(s[b * BLOCK : (b + 1) * BLOCK], axis=0, keepdims=True)
            new = jnp.maximum(new, most * EXP_SCALE - pen)
        total = jnp.zeros_like(m)
        parts = []
        for b, pen in enumerate(pens):
            p = jnp.exp2(s[b * BLOCK : (b + 1) * BLOCK] * EXP_SCALE - (new + pen))
            total = total + jnp.sum(p, axis=0, keepdims=True)
            parts.append(p.astype(bf16))
        shrink = jnp.exp2(m - new)
        m_s[i] = new
        l_s[i] = l_s[i] * shrink + total
        return shrink, jnp.concatenate(parts, axis=0)

    by_name = {"z": z_step, "x": x_step, "h": h_step}

    def all_steps(steps):
        for name, k in steps:
            by_name[name](k)

    def fold_pair(n, carry):
        for at, steps in enumerate(STEPS):
            if steps:
                pl.when(n == at)(functools.partial(all_steps, steps))
        pens = [[] for _ in range(CHUNKS)]
        keys, vt = [], []
        for e in range(2):
            rank = pick([o[0] for o in FOLD_ORDER[e::2]], n)
            col = pick([o[1] for o in FOLD_ORDER[e::2]], n)
            source = me - (NX * rank + col)
            k = jnp.where(x >= col, rank, rank + 1)
            first = jnp.maximum(source, 0) * CHUNKS
            for b in range(CHUNKS):
                key_seg = seg_ref[first + b]
                for qb in range(CHUNKS):
                    allowed = (source >= 0) & (key_seg == own_seg[qb])
                    pens[qb].append(jnp.where(allowed, 0.0, 1e30).astype(f32))
                vt.append(slots[k, col, half + b * BLOCK : half + (b + 1) * BLOCK])
            keys.append(slots[k, col, 0:half])
        keys = jnp.concatenate(keys, axis=0)
        vt = jnp.concatenate(vt, axis=1)

        def fold(t, shrink, p):
            i = t[0] * 4 + t[1]
            acc_s[i] = acc_s[i] * shrink + dot(vt, p)

        s_now = scores(keys, 0, 0)
        waiting = None
        for n_tile, t in enumerate(tiles):
            s_next = scores(keys, *tiles[n_tile + 1]) if n_tile + 1 < len(tiles) else None
            done = soft(t[0] * 4 + t[1], s_now, pens[t[0]])
            if waiting is not None:
                fold(waiting[0], *waiting[1])
            waiting = (t, done)
            s_now = s_next
        fold(waiting[0], *waiting[1])
        return carry

    lax.fori_loop(0, len(STEPS), fold_pair, 0)

    send_att = remote(tail_a, halo_a, halo_sems.at[0], halo_recv.at[0], following)
    for qb, hp in reversed(tiles):
        i = qb * 4 + hp
        o = acc_s[i] / l_s[i]
        for j in range(2):
            c = (hp * 2 + j) * HEAD_DIM
            part = o[:, j * BLOCK : (j + 1) * BLOCK].T
            att_ref[chunk(qb), c : c + HEAD_DIM] = part.astype(bf16)
        if (qb, hp) == (CHUNKS - 1, 0):
            tail_a[...] = att_ref[ROWS - 16 :, :]
            send_att.start()

    for c in (1, 2, 3, 0):
        if c == 0:
            send_att.wait_recv()
            ext[0:8] = halo_a[...].astype(f32)[8:16] * keep[c]
        else:
            before = att_ref[c * BLOCK - 16 : c * BLOCK, :]
            ext[0:8] = before.astype(f32)[8:16] * keep[c]
        ext[8:] = att_ref[chunk(c), :].astype(f32)
        conv = tap_ref[0:1, :] * ext[8 : 8 + BLOCK]
        for k in range(1, 4):
            conv = conv + tap_ref[k : k + 1, :] * ext[8 - k : 8 - k + BLOCK]
        conv = silu(conv)
        xs[chunk(c), :] = conv
        scaled = (conv * spread(heads_s[0, chunk(c), :], expand)).astype(bf16)
        write_t = cs[chunk(c), 0:STATE].T.astype(bf16)
        frag[c] = dot(write_t, scaled)
    state = frag[0]
    for c in range(1, CHUNKS):
        state = state * row_s[c : c + 1, :] + frag[c]
    for ng in range(8):
        for cg in range(4):
            s_send[ng * 4 + cg] = state[
                ng * 16 : (ng + 1) * 16, cg * 256 : (cg + 1) * 256
            ].astype(bf16)
    start_all(s_copy, NCTX, me)
    s_in[me] = s_send[me]

    low_half = lax.broadcasted_iota(jnp.int32, (BLOCK, BLOCK), 1) < SSM_DIM

    def inside(c, state):
        conv = xs[chunk(c), :]
        out = conv * row_s[CHUNKS : CHUNKS + 1, :]
        if c > 0:
            read = cs[chunk(c), STATE:].astype(bf16)
            out = out + dot(read, state.astype(bf16)) * spread(heads_s[1, chunk(c), :], expand)
        parts = []
        for pair in range(SSM_HEADS // 2):
            both = conv[:, pair * BLOCK : (pair + 1) * BLOCK]
            stacked = jnp.concatenate(
                [jnp.where(low_half, both, 0.0), jnp.where(low_half, 0.0, both)], axis=0
            ).astype(bf16)
            parts.append(dot(mix_s[c, pair], stacked))
        xs[chunk(c), :] = out + jnp.concatenate(parts, axis=1)

    state = None
    for c in range(CHUNKS):
        inside(c, state)
        state = frag[c] if c == 0 else state * row_s[c : c + 1, :] + frag[c]

    recv_all(t_copy, NCTX, me)
    share = lax.rem(me, 4)
    expand_share = jnp.where(
        lax.broadcasted_iota(jnp.int32, (BLOCK, 256), 1) // SSM_DIM + share * 4
        == lax.broadcasted_iota(jnp.int32, (BLOCK, 256), 0),
        1.0,
        0.0,
    ).astype(bf16)
    decays = spread(t_all[:, 0, :], expand_share)
    recv_all(s_copy, NCTX, me)
    running = jnp.zeros((16, 256), f32)
    for d in range(NCTX):
        p_send[d] = running.astype(bf16)
        running = running * decays[d : d + 1, :] + s_in[d].astype(f32)
    start_all(p_copy, NCTX, me)
    p_in[me] = p_send[me]
    recv_all(p_copy, NCTX, me)
    incoming = jnp.concatenate(
        [
            jnp.concatenate([p_in[ng * 4 + cg] for cg in range(4)], axis=1)
            for ng in range(8)
        ],
        axis=0,
    )
    squares = []
    for c in range(CHUNKS):
        begin = spread(heads_s[2, chunk(c), :], expand)
        out = xs[chunk(c), :] + dot(cs[chunk(c), STATE:].astype(bf16), incoming) * begin
        gated = out * gs[chunk(c), :]
        gs[chunk(c), :] = gated
        sq = gated * gated
        folded = sq[:, 0:BLOCK]
        for i in range(1, CHANNELS // BLOCK):
            folded = folded + sq[:, i * BLOCK : (i + 1) * BLOCK]
        squares.append(jnp.sum(folded.T, axis=0, keepdims=True))
    squares.append(jnp.zeros((8 - CHUNKS, BLOCK), f32))
    q_all[tp] = jnp.concatenate(squares, axis=0)
    start_all(q_copy, NTP, tp)
    recv_all(q_copy, NTP, tp)
    total = q_all[0]
    for i in range(1, NTP):
        total = total + q_all[i]
    scale = lax.rsqrt(total * (1.0 / ALL_CHANNELS) + NORM_EPS)
    for c in range(CHUNKS):
        by_row = jnp.broadcast_to(scale[c : c + 1, :], (BLOCK, BLOCK)).T
        for i in range(CHANNELS // BLOCK):
            cols = slice(i * BLOCK, (i + 1) * BLOCK)
            out_ref[chunk(c), cols] = (gs[chunk(c), cols] * gain_ref[:, cols] * by_row).astype(bf16)

    for kind, k in moves:
        act(kind, k, "wait_send")
    send_att.wait_send()
    send_proj.wait_send()
    sent_all(t_copy, NCTX, me)
    sent_all(s_copy, NCTX, me)
    sent_all(p_copy, NCTX, me)
    sent_all(q_copy, NTP, tp)


def local(
    queries, key_rows, value_rows, segments, gate_input, state_proj, step_input, step_bias,
    decay_rate, skip_gain, conv_input, conv_state, norm_gain,
):
    dma = pltpu.SemaphoreType.DMA
    vmem = pltpu.VMEM
    arrays = (
        queries.reshape(ROWS * HEADS, HEAD_DIM),
        key_rows.reshape(ROWS, HEAD_DIM),
        value_rows.reshape(ROWS, HEAD_DIM),
        gate_input,
        state_proj.reshape(2 * ROWS, STATE),
        step_input.T,
        step_bias[None, :],
        decay_rate[None, :],
        skip_gain[None, :],
        conv_input,
        conv_state.reshape(8, STATE),
        norm_gain[None, :],
    )
    return pl.pallas_call(
        layer_kernel,
        out_shape=(jax.ShapeDtypeStruct((ROWS, CHANNELS), bf16),) * 2,
        in_specs=[pl.BlockSpec(memory_space=pltpu.SMEM)]
        + [pl.BlockSpec(memory_space=pltpu.VMEM)] * len(arrays),
        out_specs=(pl.BlockSpec(memory_space=pltpu.VMEM),) * 2,
        scratch_shapes=[
            vmem((ROWS * HEADS, HEAD_DIM), f32),
            vmem((CHUNKS, HEAD_DIM, HEADS * BLOCK), bf16),
            vmem((2 * ROWS, HEAD_DIM), bf16),
            vmem((HOPS, NX, 2 * ROWS, HEAD_DIM), bf16),
            vmem((16, 1, 256), f32),
            vmem((16, 1, 256), f32),
            vmem((16, HEAD_DIM, 256), f32),
            vmem((16, CHANNELS), bf16),
            vmem((32, STATE), bf16),
            vmem((16, CHANNELS), bf16),
            vmem((32, STATE), bf16),
            vmem((8 + BLOCK, CHANNELS), f32),
            vmem((8 + BLOCK, 2 * STATE), f32),
            vmem((ROWS, CHANNELS), f32),
            vmem((ROWS, 2 * STATE), f32),
            vmem((ROWS, CHANNELS), f32),
            vmem((CHUNKS, SSM_HEADS // 2, BLOCK, 2 * BLOCK), bf16),
            vmem((CHUNKS, STATE, CHANNELS), f32),
            vmem((3, ROWS, SSM_HEADS), f32),
            vmem((8, CHANNELS), f32),
            vmem((8, BLOCK), f32),
            vmem((NCTX, 8, BLOCK), f32),
            vmem((NCTX, 16, 256), bf16),
            vmem((NCTX, 16, 256), bf16),
            vmem((NCTX, 16, 256), bf16),
            vmem((NCTX, 16, 256), bf16),
            vmem((NTP, 8, BLOCK), f32),
        ]
        + [dma((HOPS,))] * 12
        + [dma((2,)), dma((NCTX,)), dma((NCTX,)), dma((NCTX,)), dma((NTP,))] * 2,
        compiler_params=pltpu.CompilerParams(
            collective_id=0, has_side_effects=True, vmem_limit_bytes=60 << 20
        ),
        cost_estimate=pl.CostEstimate(
            flops=22 * 10**9, bytes_accessed=8 << 20, transcendentals=43 * 10**6
        ),
        name="layer",
    )(segments, *arrays)


def solution(mesh):
    placed = (
        P("ctx", "tp", None),
        P("ctx", "tp", None),
        P("ctx", "tp", None),
        P(),
        P("ctx", "tp"),
        P("ctx", None, "tp", None),
        P("ctx", "tp"),
        P("tp"),
        P("tp"),
        P("tp"),
        P(None, "tp"),
        P(None, None, "tp", None),
        P("tp"),
    )
    return jax.shard_map(
        local,
        mesh=mesh,
        in_specs=placed,
        out_specs=(P("ctx", "tp"), P("ctx", "tp")),
        check_vma=False,
    )
```

```python
import functools
import math

import jax
import jax.numpy as jnp
from jax import lax
from jax.experimental import pallas as pl
from jax.experimental.pallas import tpu as pltpu
from jax.sharding import PartitionSpec as P

BLOCK = 128
NCTX = 32
NX = 4
NZ = 8
NTP = 8
ROWS = 512
HEADS = 8
HEAD_DIM = 128
SSM_HEADS = 16
SSM_DIM = 64
CHANNELS = 1024
STATE = 128
CHUNKS = ROWS // BLOCK
ALL_CHANNELS = 8192
NORM_EPS = 1e-05
EXP_SCALE = math.log2(math.e) / math.sqrt(HEAD_DIM)
HOPS = 6
FOLD_ORDER = (
    (1, 0), (2, 0), (0, 1), (0, 3), (0, 2), (1, 1), (3, 0), (1, 3), (1, 2),
    (2, 1), (4, 0), (2, 3), (2, 2), (3, 1), (3, 3), (3, 2), (4, 1), (4, 2),
)
STEPS = (
    (),
    (("z", 3), ("h", 0), ("h", 1)),
    (("x", 2),),
    (("z", 4),),
    (("h", 2), ("x", 3)),
    (("x", 4),),
    (("h", 3), ("h", 4)),
    (),
    (("x", 5), ("h", 5)),
)

f32 = jnp.float32
bf16 = jnp.bfloat16
HIGHEST = lax.Precision.HIGHEST
MESH_ID = pl.DeviceIdType.MESH


def dot(a, b, ca=1, cb=0, precision=None):
    return lax.dot_general(
        a, b, (((ca,), (cb,)), ((), ())), precision=precision, preferred_element_type=f32
    )


def remote(src, dst, send_sem, recv_sem, device):
    return pltpu.make_async_remote_copy(
        src_ref=src,
        dst_ref=dst,
        send_sem=send_sem,
        recv_sem=recv_sem,
        device_id=device,
        device_id_type=MESH_ID,
    )


def pick(table, n):
    value = jnp.int32(table[0])
    for i in range(1, len(table)):
        value = jnp.where(n >= i, jnp.int32(table[i]), value)
    return value


def silu(v):
    return v / (1.0 + jnp.exp(-v))


def softplus(v):
    return jnp.maximum(v, 0.0) + jnp.log1p(jnp.exp(-jnp.abs(v)))


def split(v):
    high = v.astype(bf16)
    return high, (v - high.astype(f32)).astype(bf16)


def spread(v, expand):
    high, low = split(v)
    return dot(high, expand) + dot(low, expand)


def chunk(c):
    return slice(c * BLOCK, (c + 1) * BLOCK)


def layer_kernel(
    seg_ref, q_ref, k_ref, v_ref, gate_ref, proj_ref, step_ref, bias_ref, rate_ref, skip_ref,
    tap_ref, tap_state_ref, gain_ref, att_ref, out_ref,
    wide, qt, kv, slots, m_s, l_s, acc_s,
    halo_a, halo_s, tail_a, tail_s, ext, ext_s, xs, cs, gs, mix_s, frag, heads_s, row_s,
    t_send, t_all, s_send, s_in, p_send, p_in, q_all,
    send_z, send_p, send_m, send_a, send_b, send_c,
    recv_z, recv_p, recv_m, recv_a, recv_b, recv_c,
    halo_sems, t_sems, s_sems, p_sems, q_sems,
    halo_recv, t_recv, s_recv, p_recv, q_recv,
):
    me = lax.axis_index("ctx")
    tp = lax.axis_index("tp")
    z, x = me // NX, me % NX
    up = {"ctx": lax.rem(z + 1, NZ) * NX + x}
    right = {"ctx": z * NX + lax.rem(x + 1, NX)}
    left = {"ctx": z * NX + lax.rem(x + NX - 1, NX)}

    barrier = pltpu.get_barrier_semaphore()

    def greet_ctx(o, c):
        pl.semaphore_signal(
            barrier, inc=1, device_id={"ctx": lax.rem(me + o, NCTX)}, device_id_type=MESH_ID
        )
        return c

    def greet_tp(o, c):
        pl.semaphore_signal(
            barrier, inc=1, device_id={"tp": lax.rem(tp + o, NTP)}, device_id_type=MESH_ID
        )
        return c

    lax.fori_loop(1, NCTX, greet_ctx, 0)
    lax.fori_loop(1, NTP, greet_tp, 0)

    half = ROWS
    kv[0:half] = k_ref[...]
    for c in range(CHUNKS):
        kv[half + c * BLOCK : half + (c + 1) * BLOCK] = (
            v_ref[chunk(c), :].astype(f32).T.astype(bf16)
        )
    tail_s[...] = proj_ref[2 * ROWS - 32 :, :]

    pl.semaphore_wait(barrier, NCTX - 1 + NTP - 1)

    def copy_z(k):
        return remote(
            kv if k == 0 else slots.at[k, 0], slots.at[k + 1, 0], send_z.at[k], recv_z.at[k + 1], up
        )

    def copy_p(k):
        return remote(
            kv if k == 0 else slots.at[k, 0], slots.at[k, 1], send_p.at[k], recv_p.at[k], right
        )

    def copy_m(k):
        return remote(
            kv if k == 0 else slots.at[k, 0], slots.at[k, 3], send_m.at[k], recv_m.at[k], left
        )

    def copy_a(k):
        rows = pl.ds(0, 2 * half if k == 0 else half)
        return remote(
            slots.at[k, 1, rows], slots.at[k, 2, rows], send_a.at[k], recv_a.at[k], right
        )

    def copy_b(k):
        rows = pl.ds(half, half)
        return remote(
            slots.at[k, 3, rows], slots.at[k, 2, rows], send_b.at[k], recv_b.at[k], left
        )

    def copy_c(k):
        return remote(
            slots.at[k - 1, 2], slots.at[k, 2], send_c.at[k], recv_c.at[k], up
        )

    def copy_d(k):
        return remote(
            slots.at[k - 1, 1], slots.at[k, 1], send_p.at[k], recv_p.at[k], up
        )

    top = HOPS - 1
    through_z = (2,)
    always = None
    moves = {("z", k): (copy_z, always, always) for k in range(top - 1)}
    for k in range(1, top):
        moves["p", k] = (copy_p, always, always)
        moves["m", k] = (copy_m, always, always)
        if k in through_z:
            moves["c", k] = (copy_c, always, always)
        else:
            moves["a", k] = (copy_a, always, always)
            moves["b", k] = (copy_b, always, always)
    moves["p", 0] = (copy_p, x < 3, x >= 1)
    moves["m", 0] = (copy_m, x == 0, x == 3)
    moves["a", 0] = (copy_a, (x == 1) | (x == 2), x >= 2)
    moves["d", top] = (copy_d, x == 0, x == 0)
    moves["c", top] = (copy_c, x <= 1, x <= 1)

    def act(kind, k, what):
        if (kind, k) not in moves:
            return
        make, sends, receives = moves[kind, k]
        condition = receives if what == "wait_recv" else sends

        def do():
            getattr(make(k), what)()

        if condition is None:
            do()
        else:
            pl.when(condition)(do)

    def z_step(k):
        if k > 0:
            act("z", k - 1, "wait_recv")
        for kind in ("z", "p", "m"):
            act(kind, k, "start")

    def x_step(k):
        act("p", k, "wait_recv")
        act("a", k, "start")
        act("m", k, "wait_recv")
        act("b", k, "start")
        act("d", k, "wait_recv")
        act("d", k + 1, "start")

    def h_step(k):
        for kind in ("a", "b", "c"):
            act(kind, k, "wait_recv")
        act("c", k + 1, "start")

    z_step(0)

    following = {"ctx": lax.rem(me + 1, NCTX)}
    send_proj = remote(tail_s, halo_s, halo_sems.at[1], halo_recv.at[1], following)
    send_proj.start()

    def t_copy(o, slot):
        return remote(
            t_send, t_all.at[slot], t_sems, t_recv, {"ctx": lax.rem(me + o, NCTX)}
        )

    def s_copy(o, slot):
        to = lax.rem(me + o, NCTX)
        return remote(s_send.at[to], s_in.at[slot], s_sems, s_recv, {"ctx": to})

    def p_copy(o, slot):
        to = lax.rem(me + o, NCTX)
        return remote(p_send.at[to], p_in.at[slot], p_sems, p_recv, {"ctx": to})

    def q_copy(o, slot):
        return remote(
            q_all.at[tp], q_all.at[slot], q_sems, q_recv, {"tp": lax.rem(tp + o, NTP)}
        )

    def everything(buffer, sems, recv, count):
        part = buffer.at[pl.ds(0, count - 1)]
        return remote(part, part, sems, recv, following)

    exchanged = {
        t_copy: everything(t_all, t_sems, t_recv, NCTX),
        s_copy: everything(s_in, s_sems, s_recv, NCTX),
        p_copy: everything(p_in, p_sems, p_recv, NCTX),
        q_copy: everything(q_all, q_sems, q_recv, NTP),
    }

    def start_all(copy, count, place):
        def one(o, c):
            copy(o, place).start()
            return c

        lax.fori_loop(1, count, one, 0, unroll=True)

    def recv_all(copy, count, place):
        exchanged[copy].wait_recv()

    def sent_all(copy, count, place):
        exchanged[copy].wait_send()

    wide[...] = q_ref[...].astype(f32)
    for qb in range(CHUNKS):
        for h in range(HEADS):
            part = wide[pl.ds(qb * BLOCK * HEADS + h, BLOCK, stride=HEADS), :]
            qt[qb, :, h * BLOCK : (h + 1) * BLOCK] = part.T.astype(bf16)

    def scores(keys, qb, hp):
        return dot(keys, qt[qb, :, hp * 256 : (hp + 1) * 256])

    own_seg = [seg_ref[me * CHUNKS + c] for c in range(CHUNKS)]
    key_pos = lax.broadcasted_iota(jnp.int32, (BLOCK, 256), 0)
    query_pos = lax.broadcasted_iota(jnp.int32, (BLOCK, 256), 1) % BLOCK
    causal = key_pos <= query_pos
    tiles = [(qb, hp) for qb in range(CHUNKS) for hp in range(4)]

    def own_soft(qb, s):
        pens = [jnp.where(own_seg[b] == own_seg[qb], 0.0, 1e30).astype(f32) for b in range(qb)]
        last = jnp.where(causal, s[qb * BLOCK :], -1e30)
        m = jnp.max(last, axis=0, keepdims=True) * EXP_SCALE
        for b in range(qb):
            most = jnp.max(s[b * BLOCK : (b + 1) * BLOCK], axis=0, keepdims=True)
            m = jnp.maximum(m, most * EXP_SCALE - pens[b])
        total = jnp.zeros_like(m)
        parts = []
        for b in range(qb + 1):
            if b < qb:
                p = jnp.exp2(s[b * BLOCK : (b + 1) * BLOCK] * EXP_SCALE - (m + pens[b]))
            else:
                p = jnp.where(causal, jnp.exp2(last * EXP_SCALE - m), 0.0)
            total = total + jnp.sum(p, axis=0, keepdims=True)
            parts.append(p.astype(bf16))
        return m, total, jnp.concatenate(parts, axis=0)

    def values(block, count):
        return jnp.concatenate(
            [block[half + b * BLOCK : half + (b + 1) * BLOCK] for b in range(count)], axis=1
        )

    def own_fold(t, m, total, p):
        qb, hp = t
        i = qb * 4 + hp
        m_s[i] = m
        l_s[i] = total
        acc_s[i] = dot(values(kv, qb + 1), p)

    s_now = scores(kv[0:BLOCK], 0, 0)
    waiting = None
    for n, t in enumerate(tiles):
        s_next = None
        if n + 1 < len(tiles):
            qb, hp = tiles[n + 1]
            s_next = scores(kv[0 : (qb + 1) * BLOCK], qb, hp)
        done = own_soft(t[0], s_now)
        if waiting is not None:
            own_fold(waiting[0], *waiting[1])
        waiting = (t, done)
        s_now = s_next
    own_fold(waiting[0], *waiting[1])

    iota_r = lax.broadcasted_iota(jnp.int32, (BLOCK, BLOCK), 0)
    iota_c = lax.broadcasted_iota(jnp.int32, (BLOCK, BLOCK), 1)
    lower = iota_r >= iota_c
    tri = jnp.where(lower, 1.0, 0.0).astype(f32)
    expand = jnp.where(
        lax.broadcasted_iota(jnp.int32, (SSM_HEADS, CHANNELS), 1) // SSM_DIM
        == lax.broadcasted_iota(jnp.int32, (SSM_HEADS, CHANNELS), 0),
        1.0,
        0.0,
    ).astype(bf16)
    diagonal = lax.broadcasted_iota(jnp.int32, (SSM_HEADS, SSM_HEADS), 0) == (
        lax.broadcasted_iota(jnp.int32, (SSM_HEADS, SSM_HEADS), 1)
    )

    def as_column(row):
        square = jnp.broadcast_to(row, (SSM_HEADS, SSM_HEADS))
        return jnp.sum(jnp.where(diagonal, square, 0.0), axis=1, keepdims=True)

    bias = as_column(bias_ref[...])
    rate = as_column(rate_ref[...])
    keep = []
    for c in range(CHUNKS):
        at = me * CHUNKS + c
        same = (at > 0) & (seg_ref[at] == seg_ref[jnp.maximum(at - 1, 0)])
        keep.append(jnp.where(same, 1.0, 0.0).astype(f32))
    dt_t = [softplus(step_ref[:, chunk(c)] + bias) for c in range(CHUNKS)]
    cum_t = [dot(-dt_t[c] * rate, tri, 1, 1, precision=HIGHEST) for c in range(CHUNKS)]
    cum = [v.T for v in cum_t]
    last = [v[BLOCK - 1 : BLOCK, :] for v in cum]
    factor = [keep[c] * jnp.exp(last[c]) for c in range(CHUNKS)]
    prefix = [jnp.ones_like(last[0])]
    for c in range(CHUNKS):
        prefix.append(prefix[-1] * factor[c])
    t_send[...] = jnp.zeros_like(t_send)
    t_send[0:1, 0:SSM_HEADS] = prefix[CHUNKS]
    start_all(t_copy, NCTX, me)
    t_all[me] = t_send[...]
    for c in range(CHUNKS):
        begin = jnp.exp(cum[c]) * keep[c]
        heads_s[0, chunk(c), :] = jnp.exp(last[c] - cum[c]) * dt_t[c].T
        heads_s[1, chunk(c), :] = begin
        heads_s[2, chunk(c), :] = begin * prefix[c]
    rows = factor + [skip_ref[...]]
    rows = jnp.concatenate(rows + [jnp.zeros((8 - len(rows), SSM_HEADS), f32)], axis=0)
    row_s[...] = spread(rows, expand)

    send_proj.wait_recv()
    wide[0 : 2 * ROWS, :] = proj_ref[...].astype(f32)
    wide[2 * ROWS : 2 * ROWS + 32, :] = halo_s[...].astype(f32)
    for c in range(CHUNKS):
        for r in range(2):
            cols = slice(r * STATE, (r + 1) * STATE)
            first = 2 * ROWS + 16 if c == 0 else 2 * (c * BLOCK - 8)
            ext_s[0:8, cols] = wide[pl.ds(first + r, 8, stride=2), :] * keep[c]
            ext_s[8:, cols] = wide[pl.ds(2 * c * BLOCK + r, BLOCK, stride=2), :]
            conv = tap_state_ref[r : r + 1, :] * ext_s[8 : 8 + BLOCK, cols]
            for k in range(1, 4):
                tap = tap_state_ref[2 * k + r : 2 * k + r + 1, :]
                conv = conv + tap * ext_s[8 - k : 8 - k + BLOCK, cols]
            cs[chunk(c), cols] = silu(conv)
        meet = dot(cs[chunk(c), STATE:], cs[chunk(c), 0:STATE], 1, 1, precision=HIGHEST)
        for h in range(SSM_HEADS):
            gap = cum[c][:, h : h + 1] - cum_t[c][h : h + 1, :]
            mix = jnp.exp(jnp.where(lower, gap, 0.0)) * meet * dt_t[c][h : h + 1, :]
            mix_s[c, h // 2, :, (h % 2) * BLOCK : (h % 2 + 1) * BLOCK] = jnp.where(
                lower, mix, 0.0
            ).astype(bf16)
        gs[chunk(c), :] = silu(gate_ref[chunk(c), :].astype(f32))
        if c == 0:
            z_step(1)
        if c == CHUNKS - 2:
            x_step(0)
            x_step(1)
            z_step(2)

    def soft(i, s, pens):
        m = m_s[i]
        new = m
        for b, pen in enumerate(pens):
            most = jnp.max(s[b * BLOCK : (b + 1) * BLOCK], axis=0, keepdims=True)
            new = jnp.maximum(new, most * EXP_SCALE - pen)
        total = jnp.zeros_like(m)
        parts = []
        for b, pen in enumerate(pens):
            p = jnp.exp2(s[b * BLOCK : (b + 1) * BLOCK] * EXP_SCALE - (new + pen))
            total = total + jnp.sum(p, axis=0, keepdims=True)
            parts.append(p.astype(bf16))
        shrink = jnp.exp2(m - new)
        m_s[i] = new
        l_s[i] = l_s[i] * shrink + total
        return shrink, jnp.concatenate(parts, axis=0)

    by_name = {"z": z_step, "x": x_step, "h": h_step}

    def all_steps(steps):
        for name, k in steps:
            by_name[name](k)

    def fold_pair(n, carry):
        for at, steps in enumerate(STEPS):
            if steps:
                pl.when(n == at)(functools.partial(all_steps, steps))
        pens = [[] for _ in range(CHUNKS)]
        keys, vt = [], []
        for e in range(2):
            rank = pick([o[0] for o in FOLD_ORDER[e::2]], n)
            col = pick([o[1] for o in FOLD_ORDER[e::2]], n)
            source = me - (NX * rank + col)
            k = jnp.where(x >= col, rank, rank + 1)
            first = jnp.maximum(source, 0) * CHUNKS
            for b in range(CHUNKS):
                key_seg = seg_ref[first + b]
                for qb in range(CHUNKS):
                    allowed = (source >= 0) & (key_seg == own_seg[qb])
                    pens[qb].append(jnp.where(allowed, 0.0, 1e30).astype(f32))
                vt.append(slots[k, col, half + b * BLOCK : half + (b + 1) * BLOCK])
            keys.append(slots[k, col, 0:half])
        keys = jnp.concatenate(keys, axis=0)
        vt = jnp.concatenate(vt, axis=1)

        def fold(t, shrink, p):
            i = t[0] * 4 + t[1]
            acc_s[i] = acc_s[i] * shrink + dot(vt, p)

        s_now = scores(keys, 0, 0)
        waiting = None
        for n_tile, t in enumerate(tiles):
            s_next = scores(keys, *tiles[n_tile + 1]) if n_tile + 1 < len(tiles) else None
            done = soft(t[0] * 4 + t[1], s_now, pens[t[0]])
            if waiting is not None:
                fold(waiting[0], *waiting[1])
            waiting = (t, done)
            s_now = s_next
        fold(waiting[0], *waiting[1])
        return carry

    lax.fori_loop(0, len(STEPS), fold_pair, 0)

    send_att = remote(tail_a, halo_a, halo_sems.at[0], halo_recv.at[0], following)
    for qb, hp in reversed(tiles):
        i = qb * 4 + hp
        o = acc_s[i] / l_s[i]
        for j in range(2):
            c = (hp * 2 + j) * HEAD_DIM
            part = o[:, j * BLOCK : (j + 1) * BLOCK].T
            att_ref[chunk(qb), c : c + HEAD_DIM] = part.astype(bf16)
        if (qb, hp) == (CHUNKS - 1, 0):
            tail_a[...] = att_ref[ROWS - 16 :, :]
            send_att.start()

    for c in (1, 2, 3, 0):
        if c == 0:
            send_att.wait_recv()
            ext[0:8] = halo_a[...].astype(f32)[8:16] * keep[c]
        else:
            before = att_ref[c * BLOCK - 16 : c * BLOCK, :]
            ext[0:8] = before.astype(f32)[8:16] * keep[c]
        ext[8:] = att_ref[chunk(c), :].astype(f32)
        conv = tap_ref[0:1, :] * ext[8 : 8 + BLOCK]
        for k in range(1, 4):
            conv = conv + tap_ref[k : k + 1, :] * ext[8 - k : 8 - k + BLOCK]
        conv = silu(conv)
        xs[chunk(c), :] = conv
        scaled = (conv * spread(heads_s[0, chunk(c), :], expand)).astype(bf16)
        write_t = cs[chunk(c), 0:STATE].T.astype(bf16)
        frag[c] = dot(write_t, scaled)
    state = frag[0]
    for c in range(1, CHUNKS):
        state = state * row_s[c : c + 1, :] + frag[c]
    for ng in range(8):
        for cg in range(4):
            s_send[ng * 4 + cg] = state[
                ng * 16 : (ng + 1) * 16, cg * 256 : (cg + 1) * 256
            ].astype(bf16)
    start_all(s_copy, NCTX, me)
    s_in[me] = s_send[me]

    low_half = lax.broadcasted_iota(jnp.int32, (BLOCK, BLOCK), 1) < SSM_DIM

    def inside(c, state):
        conv = xs[chunk(c), :]
        out = conv * row_s[CHUNKS : CHUNKS + 1, :]
        if c > 0:
            read = cs[chunk(c), STATE:].astype(bf16)
            out = out + dot(read, state.astype(bf16)) * spread(heads_s[1, chunk(c), :], expand)
        parts = []
        for pair in range(SSM_HEADS // 2):
            both = conv[:, pair * BLOCK : (pair + 1) * BLOCK]
            stacked = jnp.concatenate(
                [jnp.where(low_half, both, 0.0), jnp.where(low_half, 0.0, both)], axis=0
            ).astype(bf16)
            parts.append(dot(mix_s[c, pair], stacked))
        xs[chunk(c), :] = out + jnp.concatenate(parts, axis=1)

    state = None
    for c in range(CHUNKS):
        inside(c, state)
        state = frag[c] if c == 0 else state * row_s[c : c + 1, :] + frag[c]

    recv_all(t_copy, NCTX, me)
    share = lax.rem(me, 4)
    expand_share = jnp.where(
        lax.broadcasted_iota(jnp.int32, (BLOCK, 256), 1) // SSM_DIM + share * 4
        == lax.broadcasted_iota(jnp.int32, (BLOCK, 256), 0),
        1.0,
        0.0,
    ).astype(bf16)
    decays = spread(t_all[:, 0, :], expand_share)
    recv_all(s_copy, NCTX, me)
    running = jnp.zeros((16, 256), f32)
    for d in range(NCTX):
        p_send[d] = running.astype(bf16)
        running = running * decays[d : d + 1, :] + s_in[d].astype(f32)
    start_all(p_copy, NCTX, me)
    p_in[me] = p_send[me]
    recv_all(p_copy, NCTX, me)
    incoming = jnp.concatenate(
        [
            jnp.concatenate([p_in[ng * 4 + cg] for cg in range(4)], axis=1)
            for ng in range(8)
        ],
        axis=0,
    )
    squares = []
    for c in range(CHUNKS):
        begin = spread(heads_s[2, chunk(c), :], expand)
        out = xs[chunk(c), :] + dot(cs[chunk(c), STATE:].astype(bf16), incoming) * begin
        gated = out * gs[chunk(c), :]
        gs[chunk(c), :] = gated
        sq = gated * gated
        folded = sq[:, 0:BLOCK]
        for i in range(1, CHANNELS // BLOCK):
            folded = folded + sq[:, i * BLOCK : (i + 1) * BLOCK]
        squares.append(jnp.sum(folded.T, axis=0, keepdims=True))
    squares.append(jnp.zeros((8 - CHUNKS, BLOCK), f32))
    q_all[tp] = jnp.concatenate(squares, axis=0)
    start_all(q_copy, NTP, tp)
    recv_all(q_copy, NTP, tp)
    total = q_all[0]
    for i in range(1, NTP):
        total = total + q_all[i]
    scale = lax.rsqrt(total * (1.0 / ALL_CHANNELS) + NORM_EPS)
    for c in range(CHUNKS):
        by_row = jnp.broadcast_to(scale[c : c + 1, :], (BLOCK, BLOCK)).T
        for i in range(CHANNELS // BLOCK):
            cols = slice(i * BLOCK, (i + 1) * BLOCK)
            out_ref[chunk(c), cols] = (gs[chunk(c), cols] * gain_ref[:, cols] * by_row).astype(bf16)

    for kind, k in moves:
        act(kind, k, "wait_send")
    send_att.wait_send()
    send_proj.wait_send()
    sent_all(t_copy, NCTX, me)
    sent_all(s_copy, NCTX, me)
    sent_all(p_copy, NCTX, me)
    sent_all(q_copy, NTP, tp)


def local(
    queries, key_rows, value_rows, segments, gate_input, state_proj, step_input, step_bias,
    decay_rate, skip_gain, conv_input, conv_state, norm_gain,
):
    dma = pltpu.SemaphoreType.DMA
    vmem = pltpu.VMEM
    arrays = (
        queries.reshape(ROWS * HEADS, HEAD_DIM),
        key_rows.reshape(ROWS, HEAD_DIM),
        value_rows.reshape(ROWS, HEAD_DIM),
        gate_input,
        state_proj.reshape(2 * ROWS, STATE),
        step_input.T,
        step_bias[None, :],
        decay_rate[None, :],
        skip_gain[None, :],
        conv_input,
        conv_state.reshape(8, STATE),
        norm_gain[None, :],
    )
    return pl.pallas_call(
        layer_kernel,
        out_shape=(jax.ShapeDtypeStruct((ROWS, CHANNELS), bf16),) * 2,
        in_specs=[pl.BlockSpec(memory_space=pltpu.SMEM)]
        + [pl.BlockSpec(memory_space=pltpu.VMEM)] * len(arrays),
        out_specs=(pl.BlockSpec(memory_space=pltpu.VMEM),) * 2,
        scratch_shapes=[
            vmem((ROWS * HEADS, HEAD_DIM), f32),
            vmem((CHUNKS, HEAD_DIM, HEADS * BLOCK), bf16),
            vmem((2 * ROWS, HEAD_DIM), bf16),
            vmem((HOPS, NX, 2 * ROWS, HEAD_DIM), bf16),
            vmem((16, 1, 256), f32),
            vmem((16, 1, 256), f32),
            vmem((16, HEAD_DIM, 256), f32),
            vmem((16, CHANNELS), bf16),
            vmem((32, STATE), bf16),
            vmem((16, CHANNELS), bf16),
            vmem((32, STATE), bf16),
            vmem((8 + BLOCK, CHANNELS), f32),
            vmem((8 + BLOCK, 2 * STATE), f32),
            vmem((ROWS, CHANNELS), f32),
            vmem((ROWS, 2 * STATE), f32),
            vmem((ROWS, CHANNELS), f32),
            vmem((CHUNKS, SSM_HEADS // 2, BLOCK, 2 * BLOCK), bf16),
            vmem((CHUNKS, STATE, CHANNELS), f32),
            vmem((3, ROWS, SSM_HEADS), f32),
            vmem((8, CHANNELS), f32),
            vmem((8, BLOCK), f32),
            vmem((NCTX, 8, BLOCK), f32),
            vmem((NCTX, 16, 256), bf16),
            vmem((NCTX, 16, 256), bf16),
            vmem((NCTX, 16, 256), bf16),
            vmem((NCTX, 16, 256), bf16),
            vmem((NTP, 8, BLOCK), f32),
        ]
        + [dma((HOPS,))] * 12
        + [dma((2,)), dma(()), dma(()), dma(()), dma(())] * 2,
        compiler_params=pltpu.CompilerParams(
            collective_id=0, has_side_effects=True, vmem_limit_bytes=60 << 20
        ),
        cost_estimate=pl.CostEstimate(
            flops=22 * 10**9, bytes_accessed=8 << 20, transcendentals=43 * 10**6
        ),
        name="layer",
    )(segments, *arrays)


def solution(mesh):
    placed = (
        P("ctx", "tp", None),
        P("ctx", "tp", None),
        P("ctx", "tp", None),
        P(),
        P("ctx", "tp"),
        P("ctx", None, "tp", None),
        P("ctx", "tp"),
        P("tp"),
        P("tp"),
        P("tp"),
        P(None, "tp"),
        P(None, None, "tp", None),
        P("tp"),
    )
    return jax.shard_map(
        local,
        mesh=mesh,
        in_specs=placed,
        out_specs=(P("ctx", "tp"), P("ctx", "tp")),
        check_vma=False,
    )
```

```python
import functools
import math

import jax
import jax.numpy as jnp
from jax import lax
from jax.experimental import pallas as pl
from jax.experimental.pallas import tpu as pltpu
from jax.sharding import PartitionSpec as P

BLOCK = 128
NCTX = 32
NX = 4
NZ = 8
NTP = 8
ROWS = 512
HEADS = 8
HEAD_DIM = 128
SSM_HEADS = 16
SSM_DIM = 64
CHANNELS = 1024
STATE = 128
CHUNKS = ROWS // BLOCK
ALL_CHANNELS = 8192
NORM_EPS = 1e-05
EXP_SCALE = math.log2(math.e) / math.sqrt(HEAD_DIM)
HOPS = 6
FOLD_ORDER = (
    (1, 0), (2, 0), (0, 1), (0, 3), (0, 2), (1, 1), (3, 0), (1, 3), (1, 2),
    (2, 1), (4, 0), (2, 3), (2, 2), (3, 1), (3, 3), (3, 2), (4, 1), (4, 2),
)
STEPS = (
    (),
    (("z", 3),),
    (("x", 2), ("h", 0), ("h", 1)),
    (("z", 4),),
    (("h", 2), ("x", 3)),
    (("x", 4),),
    (("h", 3), ("h", 4)),
    (),
    (("x", 5), ("h", 5)),
)

f32 = jnp.float32
bf16 = jnp.bfloat16
HIGHEST = lax.Precision.HIGHEST
MESH_ID = pl.DeviceIdType.MESH


def dot(a, b, ca=1, cb=0, precision=None):
    return lax.dot_general(
        a, b, (((ca,), (cb,)), ((), ())), precision=precision, preferred_element_type=f32
    )


def remote(src, dst, send_sem, recv_sem, device):
    return pltpu.make_async_remote_copy(
        src_ref=src,
        dst_ref=dst,
        send_sem=send_sem,
        recv_sem=recv_sem,
        device_id=device,
        device_id_type=MESH_ID,
    )


def pick(table, n):
    value = jnp.int32(table[0])
    for i in range(1, len(table)):
        value = jnp.where(n >= i, jnp.int32(table[i]), value)
    return value


def silu(v):
    return v / (1.0 + jnp.exp(-v))


def softplus(v):
    return jnp.maximum(v, 0.0) + jnp.log1p(jnp.exp(-jnp.abs(v)))


def split(v):
    high = v.astype(bf16)
    return high, (v - high.astype(f32)).astype(bf16)


def spread(v, expand):
    high, low = split(v)
    return dot(high, expand) + dot(low, expand)


def chunk(c):
    return slice(c * BLOCK, (c + 1) * BLOCK)


def layer_kernel(
    seg_ref, q_ref, k_ref, v_ref, gate_ref, proj_ref, step_ref, bias_ref, rate_ref, skip_ref,
    tap_ref, tap_state_ref, gain_ref, att_ref, out_ref,
    wide, qt, kv, slots, m_s, l_s, acc_s,
    halo_a, halo_s, tail_a, tail_s, ext, ext_s, xs, cs, gs, mix_s, frag, heads_s, row_s,
    t_send, t_all, s_send, s_in, p_send, p_in, q_all,
    send_z, send_p, send_m, send_a, send_b, send_c,
    recv_z, recv_p, recv_m, recv_a, recv_b, recv_c,
    halo_sems, t_sems, s_sems, p_sems, q_sems,
    halo_recv, t_recv, s_recv, p_recv, q_recv,
):
    me = lax.axis_index("ctx")
    tp = lax.axis_index("tp")
    z, x = me // NX, me % NX
    up = {"ctx": lax.rem(z + 1, NZ) * NX + x}
    right = {"ctx": z * NX + lax.rem(x + 1, NX)}
    left = {"ctx": z * NX + lax.rem(x + NX - 1, NX)}

    barrier = pltpu.get_barrier_semaphore()

    def greet_ctx(o, c):
        pl.semaphore_signal(
            barrier, inc=1, device_id={"ctx": lax.rem(me + o, NCTX)}, device_id_type=MESH_ID
        )
        return c

    def greet_tp(o, c):
        pl.semaphore_signal(
            barrier, inc=1, device_id={"tp": lax.rem(tp + o, NTP)}, device_id_type=MESH_ID
        )
        return c

    lax.fori_loop(1, NCTX, greet_ctx, 0)
    lax.fori_loop(1, NTP, greet_tp, 0)

    half = ROWS
    kv[0:half] = k_ref[...]
    for c in range(CHUNKS):
        kv[half + c * BLOCK : half + (c + 1) * BLOCK] = (
            v_ref[chunk(c), :].astype(f32).T.astype(bf16)
        )
    tail_s[...] = proj_ref[2 * ROWS - 32 :, :]

    pl.semaphore_wait(barrier, NCTX - 1 + NTP - 1)

    def copy_z(k):
        return remote(
            kv if k == 0 else slots.at[k, 0], slots.at[k + 1, 0], send_z.at[k], recv_z.at[k + 1], up
        )

    def copy_p(k):
        return remote(
            kv if k == 0 else slots.at[k, 0], slots.at[k, 1], send_p.at[k], recv_p.at[k], right
        )

    def copy_m(k):
        return remote(
            kv if k == 0 else slots.at[k, 0], slots.at[k, 3], send_m.at[k], recv_m.at[k], left
        )

    def copy_a(k):
        rows = pl.ds(0, 2 * half if k == 0 else half)
        return remote(
            slots.at[k, 1, rows], slots.at[k, 2, rows], send_a.at[k], recv_a.at[k], right
        )

    def copy_b(k):
        rows = pl.ds(half, half)
        return remote(
            slots.at[k, 3, rows], slots.at[k, 2, rows], send_b.at[k], recv_b.at[k], left
        )

    def copy_c(k):
        return remote(
            slots.at[k - 1, 2], slots.at[k, 2], send_c.at[k], recv_c.at[k], up
        )

    def copy_d(k):
        return remote(
            slots.at[k - 1, 1], slots.at[k, 1], send_p.at[k], recv_p.at[k], up
        )

    top = HOPS - 1
    through_z = (2,)
    always = None
    moves = {("z", k): (copy_z, always, always) for k in range(top - 1)}
    for k in range(1, top):
        moves["p", k] = (copy_p, always, always)
        moves["m", k] = (copy_m, always, always)
        if k in through_z:
            moves["c", k] = (copy_c, always, always)
        else:
            moves["a", k] = (copy_a, always, always)
            moves["b", k] = (copy_b, always, always)
    moves["p", 0] = (copy_p, x < 3, x >= 1)
    moves["m", 0] = (copy_m, x == 0, x == 3)
    moves["a", 0] = (copy_a, (x == 1) | (x == 2), x >= 2)
    moves["d", top] = (copy_d, x == 0, x == 0)
    moves["c", top] = (copy_c, x <= 1, x <= 1)

    def act(kind, k, what):
        if (kind, k) not in moves:
            return
        make, sends, receives = moves[kind, k]
        row = k + 1 if kind == "z" else k
        if what == "wait_recv":
            condition, inside = receives, z >= row
        else:
            condition = sends
            inside = z >= k if kind in "pmab" else z + 1 >= row
            if kind in "zcd":
                inside = inside & (z < NZ - 1)
        condition = inside if condition is None else condition & inside

        def do():
            getattr(make(k), what)()

        if condition is None:
            do()
        else:
            pl.when(condition)(do)

    def z_step(k):
        if k > 0:
            act("z", k - 1, "wait_recv")
        for kind in ("z", "p", "m"):
            act(kind, k, "start")

    def x_step(k):
        act("p", k, "wait_recv")
        act("a", k, "start")
        act("m", k, "wait_recv")
        act("b", k, "start")
        act("d", k, "wait_recv")
        act("d", k + 1, "start")

    def h_step(k):
        for kind in ("a", "b", "c"):
            act(kind, k, "wait_recv")
        act("c", k + 1, "start")

    for k in range(1, HOPS):

        def clear(k=k):
            slots[k] = jnp.zeros(slots.shape[1:], bf16)

        pl.when(z < k)(clear)

    z_step(0)

    following = {"ctx": lax.rem(me + 1, NCTX)}
    send_proj = remote(tail_s, halo_s, halo_sems.at[1], halo_recv.at[1], following)
    send_proj.start()

    def t_copy(o, slot):
        return remote(
            t_send, t_all.at[slot], t_sems, t_recv, {"ctx": lax.rem(me + o, NCTX)}
        )

    def s_copy(o, slot):
        to = lax.rem(me + o, NCTX)
        return remote(s_send.at[to], s_in.at[slot], s_sems, s_recv, {"ctx": to})

    def p_copy(o, slot):
        to = lax.rem(me + o, NCTX)
        return remote(p_send.at[to], p_in.at[slot], p_sems, p_recv, {"ctx": to})

    def q_copy(o, slot):
        return remote(
            q_all.at[tp], q_all.at[slot], q_sems, q_recv, {"tp": lax.rem(tp + o, NTP)}
        )

    def everything(buffer, sems, recv, count):
        part = buffer.at[pl.ds(0, count - 1)]
        return remote(part, part, sems, recv, following)

    exchanged = {
        t_copy: everything(t_all, t_sems, t_recv, NCTX),
        s_copy: everything(s_in, s_sems, s_recv, NCTX),
        p_copy: everything(p_in, p_sems, p_recv, NCTX),
        q_copy: everything(q_all, q_sems, q_recv, NTP),
    }

    def start_all(copy, count, place):
        def one(o, c):
            copy(o, place).start()
            return c

        lax.fori_loop(1, count, one, 0, unroll=True)

    def recv_all(copy, count, place):
        exchanged[copy].wait_recv()

    def sent_all(copy, count, place):
        exchanged[copy].wait_send()

    wide[...] = q_ref[...].astype(f32)
    for qb in range(CHUNKS):
        for h in range(HEADS):
            part = wide[pl.ds(qb * BLOCK * HEADS + h, BLOCK, stride=HEADS), :]
            qt[qb, :, h * BLOCK : (h + 1) * BLOCK] = part.T.astype(bf16)

    def scores(keys, qb, hp):
        return dot(keys, qt[qb, :, hp * 256 : (hp + 1) * 256])

    own_seg = [seg_ref[me * CHUNKS + c] for c in range(CHUNKS)]
    key_pos = lax.broadcasted_iota(jnp.int32, (BLOCK, 256), 0)
    query_pos = lax.broadcasted_iota(jnp.int32, (BLOCK, 256), 1) % BLOCK
    causal = key_pos <= query_pos
    tiles = [(qb, hp) for qb in range(CHUNKS) for hp in range(4)]

    def own_soft(qb, s):
        pens = [jnp.where(own_seg[b] == own_seg[qb], 0.0, 1e30).astype(f32) for b in range(qb)]
        last = jnp.where(causal, s[qb * BLOCK :], -1e30)
        m = jnp.max(last, axis=0, keepdims=True) * EXP_SCALE
        for b in range(qb):
            most = jnp.max(s[b * BLOCK : (b + 1) * BLOCK], axis=0, keepdims=True)
            m = jnp.maximum(m, most * EXP_SCALE - pens[b])
        total = jnp.zeros_like(m)
        parts = []
        for b in range(qb + 1):
            if b < qb:
                p = jnp.exp2(s[b * BLOCK : (b + 1) * BLOCK] * EXP_SCALE - (m + pens[b]))
            else:
                p = jnp.where(causal, jnp.exp2(last * EXP_SCALE - m), 0.0)
            total = total + jnp.sum(p, axis=0, keepdims=True)
            parts.append(p.astype(bf16))
        return m, total, jnp.concatenate(parts, axis=0)

    def values(block, count):
        return jnp.concatenate(
            [block[half + b * BLOCK : half + (b + 1) * BLOCK] for b in range(count)], axis=1
        )

    def own_fold(t, m, total, p):
        qb, hp = t
        i = qb * 4 + hp
        m_s[i] = m
        l_s[i] = total
        acc_s[i] = dot(values(kv, qb + 1), p)

    s_now = scores(kv[0:BLOCK], 0, 0)
    waiting = None
    for n, t in enumerate(tiles):
        s_next = None
        if n + 1 < len(tiles):
            qb, hp = tiles[n + 1]
            s_next = scores(kv[0 : (qb + 1) * BLOCK], qb, hp)
        done = own_soft(t[0], s_now)
        if waiting is not None:
            own_fold(waiting[0], *waiting[1])
        waiting = (t, done)
        s_now = s_next
    own_fold(waiting[0], *waiting[1])

    iota_r = lax.broadcasted_iota(jnp.int32, (BLOCK, BLOCK), 0)
    iota_c = lax.broadcasted_iota(jnp.int32, (BLOCK, BLOCK), 1)
    lower = iota_r >= iota_c
    tri = jnp.where(lower, 1.0, 0.0).astype(f32)
    expand = jnp.where(
        lax.broadcasted_iota(jnp.int32, (SSM_HEADS, CHANNELS), 1) // SSM_DIM
        == lax.broadcasted_iota(jnp.int32, (SSM_HEADS, CHANNELS), 0),
        1.0,
        0.0,
    ).astype(bf16)
    diagonal = lax.broadcasted_iota(jnp.int32, (SSM_HEADS, SSM_HEADS), 0) == (
        lax.broadcasted_iota(jnp.int32, (SSM_HEADS, SSM_HEADS), 1)
    )

    def as_column(row):
        square = jnp.broadcast_to(row, (SSM_HEADS, SSM_HEADS))
        return jnp.sum(jnp.where(diagonal, square, 0.0), axis=1, keepdims=True)

    bias = as_column(bias_ref[...])
    rate = as_column(rate_ref[...])
    keep = []
    for c in range(CHUNKS):
        at = me * CHUNKS + c
        same = (at > 0) & (seg_ref[at] == seg_ref[jnp.maximum(at - 1, 0)])
        keep.append(jnp.where(same, 1.0, 0.0).astype(f32))
    dt_t = [softplus(step_ref[:, chunk(c)] + bias) for c in range(CHUNKS)]
    cum_t = [dot(-dt_t[c] * rate, tri, 1, 1, precision=HIGHEST) for c in range(CHUNKS)]
    cum = [v.T for v in cum_t]
    last = [v[BLOCK - 1 : BLOCK, :] for v in cum]
    factor = [keep[c] * jnp.exp(last[c]) for c in range(CHUNKS)]
    prefix = [jnp.ones_like(last[0])]
    for c in range(CHUNKS):
        prefix.append(prefix[-1] * factor[c])
    t_send[...] = jnp.zeros_like(t_send)
    t_send[0:1, 0:SSM_HEADS] = prefix[CHUNKS]
    start_all(t_copy, NCTX, me)
    t_all[me] = t_send[...]
    for c in range(CHUNKS):
        begin = jnp.exp(cum[c]) * keep[c]
        heads_s[0, chunk(c), :] = jnp.exp(last[c] - cum[c]) * dt_t[c].T
        heads_s[1, chunk(c), :] = begin
        heads_s[2, chunk(c), :] = begin * prefix[c]
    rows = factor + [skip_ref[...]]
    rows = jnp.concatenate(rows + [jnp.zeros((8 - len(rows), SSM_HEADS), f32)], axis=0)
    row_s[...] = spread(rows, expand)

    send_proj.wait_recv()
    wide[0 : 2 * ROWS, :] = proj_ref[...].astype(f32)
    wide[2 * ROWS : 2 * ROWS + 32, :] = halo_s[...].astype(f32)
    for c in range(CHUNKS):
        for r in range(2):
            cols = slice(r * STATE, (r + 1) * STATE)
            first = 2 * ROWS + 16 if c == 0 else 2 * (c * BLOCK - 8)
            ext_s[0:8, cols] = wide[pl.ds(first + r, 8, stride=2), :] * keep[c]
            ext_s[8:, cols] = wide[pl.ds(2 * c * BLOCK + r, BLOCK, stride=2), :]
            conv = tap_state_ref[r : r + 1, :] * ext_s[8 : 8 + BLOCK, cols]
            for k in range(1, 4):
                tap = tap_state_ref[2 * k + r : 2 * k + r + 1, :]
                conv = conv + tap * ext_s[8 - k : 8 - k + BLOCK, cols]
            cs[chunk(c), cols] = silu(conv)
        meet = dot(cs[chunk(c), STATE:], cs[chunk(c), 0:STATE], 1, 1, precision=HIGHEST)
        for h in range(SSM_HEADS):
            gap = cum[c][:, h : h + 1] - cum_t[c][h : h + 1, :]
            mix = jnp.exp(jnp.where(lower, gap, 0.0)) * meet * dt_t[c][h : h + 1, :]
            mix_s[c, h // 2, :, (h % 2) * BLOCK : (h % 2 + 1) * BLOCK] = jnp.where(
                lower, mix, 0.0
            ).astype(bf16)
        gs[chunk(c), :] = silu(gate_ref[chunk(c), :].astype(f32))
        if c == 0:
            z_step(1)
        if c == CHUNKS - 2:
            x_step(0)
            x_step(1)
            z_step(2)

    def soft(i, s, pens):
        m = m_s[i]
        new = m
        for b, pen in enumerate(pens):
            most = jnp.max(s[b * BLOCK : (b + 1) * BLOCK], axis=0, keepdims=True)
            new = jnp.maximum(new, most * EXP_SCALE - pen)
        total = jnp.zeros_like(m)
        parts = []
        for b, pen in enumerate(pens):
            p = jnp.exp2(s[b * BLOCK : (b + 1) * BLOCK] * EXP_SCALE - (new + pen))
            total = total + jnp.sum(p, axis=0, keepdims=True)
            parts.append(p.astype(bf16))
        shrink = jnp.exp2(m - new)
        m_s[i] = new
        l_s[i] = l_s[i] * shrink + total
        return shrink, jnp.concatenate(parts, axis=0)

    by_name = {"z": z_step, "x": x_step, "h": h_step}

    def all_steps(steps):
        for name, k in steps:
            by_name[name](k)

    def fold_pair(n, carry):
        for at, steps in enumerate(STEPS):
            if steps:
                pl.when(n == at)(functools.partial(all_steps, steps))
        pens = [[] for _ in range(CHUNKS)]
        keys, vt = [], []
        for e in range(2):
            rank = pick([o[0] for o in FOLD_ORDER[e::2]], n)
            col = pick([o[1] for o in FOLD_ORDER[e::2]], n)
            source = me - (NX * rank + col)
            k = jnp.where(x >= col, rank, rank + 1)
            first = jnp.maximum(source, 0) * CHUNKS
            for b in range(CHUNKS):
                key_seg = seg_ref[first + b]
                for qb in range(CHUNKS):
                    allowed = (source >= 0) & (key_seg == own_seg[qb])
                    pens[qb].append(jnp.where(allowed, 0.0, 1e30).astype(f32))
                vt.append(slots[k, col, half + b * BLOCK : half + (b + 1) * BLOCK])
            keys.append(slots[k, col, 0:half])
        keys = jnp.concatenate(keys, axis=0)
        vt = jnp.concatenate(vt, axis=1)

        def fold(t, shrink, p):
            i = t[0] * 4 + t[1]
            acc_s[i] = acc_s[i] * shrink + dot(vt, p)

        s_now = scores(keys, 0, 0)
        waiting = None
        for n_tile, t in enumerate(tiles):
            s_next = scores(keys, *tiles[n_tile + 1]) if n_tile + 1 < len(tiles) else None
            done = soft(t[0] * 4 + t[1], s_now, pens[t[0]])
            if waiting is not None:
                fold(waiting[0], *waiting[1])
            waiting = (t, done)
            s_now = s_next
        fold(waiting[0], *waiting[1])
        return carry

    lax.fori_loop(0, len(STEPS), fold_pair, 0)

    send_att = remote(tail_a, halo_a, halo_sems.at[0], halo_recv.at[0], following)
    for qb, hp in reversed(tiles):
        i = qb * 4 + hp
        o = acc_s[i] / l_s[i]
        for j in range(2):
            c = (hp * 2 + j) * HEAD_DIM
            part = o[:, j * BLOCK : (j + 1) * BLOCK].T
            att_ref[chunk(qb), c : c + HEAD_DIM] = part.astype(bf16)
        if (qb, hp) == (CHUNKS - 1, 0):
            tail_a[...] = att_ref[ROWS - 16 :, :]
            send_att.start()

    for c in (1, 2, 3, 0):
        if c == 0:
            send_att.wait_recv()
            ext[0:8] = halo_a[...].astype(f32)[8:16] * keep[c]
        else:
            before = att_ref[c * BLOCK - 16 : c * BLOCK, :]
            ext[0:8] = before.astype(f32)[8:16] * keep[c]
        ext[8:] = att_ref[chunk(c), :].astype(f32)
        conv = tap_ref[0:1, :] * ext[8 : 8 + BLOCK]
        for k in range(1, 4):
            conv = conv + tap_ref[k : k + 1, :] * ext[8 - k : 8 - k + BLOCK]
        conv = silu(conv)
        xs[chunk(c), :] = conv
        scaled = (conv * spread(heads_s[0, chunk(c), :], expand)).astype(bf16)
        write_t = cs[chunk(c), 0:STATE].T.astype(bf16)
        frag[c] = dot(write_t, scaled)
    state = frag[0]
    for c in range(1, CHUNKS):
        state = state * row_s[c : c + 1, :] + frag[c]
    for ng in range(8):
        for cg in range(4):
            s_send[ng * 4 + cg] = state[
                ng * 16 : (ng + 1) * 16, cg * 256 : (cg + 1) * 256
            ].astype(bf16)
    start_all(s_copy, NCTX, me)
    s_in[me] = s_send[me]

    low_half = lax.broadcasted_iota(jnp.int32, (BLOCK, BLOCK), 1) < SSM_DIM

    def inside(c, state):
        conv = xs[chunk(c), :]
        out = conv * row_s[CHUNKS : CHUNKS + 1, :]
        if c > 0:
            read = cs[chunk(c), STATE:].astype(bf16)
            out = out + dot(read, state.astype(bf16)) * spread(heads_s[1, chunk(c), :], expand)
        parts = []
        for pair in range(SSM_HEADS // 2):
            both = conv[:, pair * BLOCK : (pair + 1) * BLOCK]
            stacked = jnp.concatenate(
                [jnp.where(low_half, both, 0.0), jnp.where(low_half, 0.0, both)], axis=0
            ).astype(bf16)
            parts.append(dot(mix_s[c, pair], stacked))
        xs[chunk(c), :] = out + jnp.concatenate(parts, axis=1)

    state = frag[0]
    inside(0, None)
    for c in range(1, 2):
        inside(c, state)
        state = state * row_s[c : c + 1, :] + frag[c]

    recv_all(t_copy, NCTX, me)
    share = lax.rem(me, 4)
    expand_share = jnp.where(
        lax.broadcasted_iota(jnp.int32, (BLOCK, 256), 1) // SSM_DIM + share * 4
        == lax.broadcasted_iota(jnp.int32, (BLOCK, 256), 0),
        1.0,
        0.0,
    ).astype(bf16)
    decays = spread(t_all[:, 0, :], expand_share)
    recv_all(s_copy, NCTX, me)
    running = jnp.zeros((16, 256), f32)
    for d in range(NCTX):
        p_send[d] = running.astype(bf16)
        running = running * decays[d : d + 1, :] + s_in[d].astype(f32)
    start_all(p_copy, NCTX, me)
    p_in[me] = p_send[me]
    for c in range(2, CHUNKS):
        inside(c, state)
        state = state * row_s[c : c + 1, :] + frag[c]
    recv_all(p_copy, NCTX, me)
    incoming = jnp.concatenate(
        [
            jnp.concatenate([p_in[ng * 4 + cg] for cg in range(4)], axis=1)
            for ng in range(8)
        ],
        axis=0,
    )
    squares = []
    for c in range(CHUNKS):
        begin = spread(heads_s[2, chunk(c), :], expand)
        out = xs[chunk(c), :] + dot(cs[chunk(c), STATE:].astype(bf16), incoming) * begin
        gated = out * gs[chunk(c), :]
        gs[chunk(c), :] = gated
        sq = gated * gated
        folded = sq[:, 0:BLOCK]
        for i in range(1, CHANNELS // BLOCK):
            folded = folded + sq[:, i * BLOCK : (i + 1) * BLOCK]
        squares.append(jnp.sum(folded.T, axis=0, keepdims=True))
    squares.append(jnp.zeros((8 - CHUNKS, BLOCK), f32))
    q_all[tp] = jnp.concatenate(squares, axis=0)
    start_all(q_copy, NTP, tp)
    recv_all(q_copy, NTP, tp)
    total = q_all[0]
    for i in range(1, NTP):
        total = total + q_all[i]
    scale = lax.rsqrt(total * (1.0 / ALL_CHANNELS) + NORM_EPS)
    for c in range(CHUNKS):
        by_row = jnp.broadcast_to(scale[c : c + 1, :], (BLOCK, BLOCK)).T
        for i in range(CHANNELS // BLOCK):
            cols = slice(i * BLOCK, (i + 1) * BLOCK)
            out_ref[chunk(c), cols] = (gs[chunk(c), cols] * gain_ref[:, cols] * by_row).astype(bf16)

    for kind, k in moves:
        act(kind, k, "wait_send")
    send_att.wait_send()
    send_proj.wait_send()
    sent_all(t_copy, NCTX, me)
    sent_all(s_copy, NCTX, me)
    sent_all(p_copy, NCTX, me)
    sent_all(q_copy, NTP, tp)


def local(
    queries, key_rows, value_rows, segments, gate_input, state_proj, step_input, step_bias,
    decay_rate, skip_gain, conv_input, conv_state, norm_gain,
):
    dma = pltpu.SemaphoreType.DMA
    vmem = pltpu.VMEM
    arrays = (
        queries.reshape(ROWS * HEADS, HEAD_DIM),
        key_rows.reshape(ROWS, HEAD_DIM),
        value_rows.reshape(ROWS, HEAD_DIM),
        gate_input,
        state_proj.reshape(2 * ROWS, STATE),
        step_input.T,
        step_bias[None, :],
        decay_rate[None, :],
        skip_gain[None, :],
        conv_input,
        conv_state.reshape(8, STATE),
        norm_gain[None, :],
    )
    return pl.pallas_call(
        layer_kernel,
        out_shape=(jax.ShapeDtypeStruct((ROWS, CHANNELS), bf16),) * 2,
        in_specs=[pl.BlockSpec(memory_space=pltpu.SMEM)]
        + [pl.BlockSpec(memory_space=pltpu.VMEM)] * len(arrays),
        out_specs=(pl.BlockSpec(memory_space=pltpu.VMEM),) * 2,
        scratch_shapes=[
            vmem((ROWS * HEADS, HEAD_DIM), f32),
            vmem((CHUNKS, HEAD_DIM, HEADS * BLOCK), bf16),
            vmem((2 * ROWS, HEAD_DIM), bf16),
            vmem((HOPS, NX, 2 * ROWS, HEAD_DIM), bf16),
            vmem((16, 1, 256), f32),
            vmem((16, 1, 256), f32),
            vmem((16, HEAD_DIM, 256), f32),
            vmem((16, CHANNELS), bf16),
            vmem((32, STATE), bf16),
            vmem((16, CHANNELS), bf16),
            vmem((32, STATE), bf16),
            vmem((8 + BLOCK, CHANNELS), f32),
            vmem((8 + BLOCK, 2 * STATE), f32),
            vmem((ROWS, CHANNELS), f32),
            vmem((ROWS, 2 * STATE), f32),
            vmem((ROWS, CHANNELS), f32),
            vmem((CHUNKS, SSM_HEADS // 2, BLOCK, 2 * BLOCK), bf16),
            vmem((CHUNKS, STATE, CHANNELS), f32),
            vmem((3, ROWS, SSM_HEADS), f32),
            vmem((8, CHANNELS), f32),
            vmem((8, BLOCK), f32),
            vmem((NCTX, 8, BLOCK), f32),
            vmem((NCTX, 16, 256), bf16),
            vmem((NCTX, 16, 256), bf16),
            vmem((NCTX, 16, 256), bf16),
            vmem((NCTX, 16, 256), bf16),
            vmem((NTP, 8, BLOCK), f32),
        ]
        + [dma((HOPS,))] * 12
        + [dma((2,)), dma(()), dma(()), dma(()), dma(())] * 2,
        compiler_params=pltpu.CompilerParams(
            collective_id=0, has_side_effects=True, vmem_limit_bytes=60 << 20
        ),
        cost_estimate=pl.CostEstimate(
            flops=22 * 10**9, bytes_accessed=8 << 20, transcendentals=43 * 10**6
        ),
        name="layer",
    )(segments, *arrays)


def solution(mesh):
    placed = (
        P("ctx", "tp", None),
        P("ctx", "tp", None),
        P("ctx", "tp", None),
        P(),
        P("ctx", "tp"),
        P("ctx", None, "tp", None),
        P("ctx", "tp"),
        P("tp"),
        P("tp"),
        P("tp"),
        P(None, "tp"),
        P(None, None, "tp", None),
        P("tp"),
    )
    return jax.shard_map(
        local,
        mesh=mesh,
        in_specs=placed,
        out_specs=(P("ctx", "tp"), P("ctx", "tp")),
        check_vma=False,
    )
```
